256 devices in a mesh: img: 32 (over z, x), txt: 8 (over y, core).
Axes of the slice: x: 4, y: 4, z: 8, core: 2. Of those that a mesh axis runs over, the one named last changes fastest.
Arguments:
- picture_vectors: float32 [16384, 1152], P(('img', 'txt')), may hold values from -0.2 to 0.2
- caption_vectors: float32 [16384, 1152], P(('txt', 'img')), may hold values from -0.2 to 0.2
- warmth_exponent: float32 [1], replicated, may hold values from 3 to 3.7
- offset_weight: float32 [1], replicated, may hold values from -8 to -5
Outputs:
- mean_sigmoid_penalty: float32 [1], replicated
- picture_derivative: float32 [16384, 1152], P(('img', 'txt'))
- caption_derivative: float32 [16384, 1152], P(('txt', 'img'))
- warmth_derivative: float32 [1], replicated
- offset_derivative: float32 [1], replicated
The draws below stay inside these ranges and needn't reach their ends.
All inputs are finite; a program needn't handle non-finite values.
Results may differ from the reference program's by a relative error of at most 0.0003.
Values sent between devices are 32-bit elements; how exact they have to be, the bound alone decides.
A program may use at most 128 MiB of HBM per device.

```python
import math
import jax
import jax.numpy as jnp
from jax import lax

D = 1152
MATCHED_ROWS_NUM = 16384


def level_of(stream_key, dims, pieces, smallest, top_value):
    loudness = 1.0
    for axis_at, shards_of in pieces:
        draws = jax.random.uniform(jax.random.fold_in(jax.random.fold_in(stream_key, 6), axis_at), (shards_of,), jnp.float32, smallest / len(pieces), top_value / len(pieces))
        loudness = loudness * jnp.repeat(jnp.exp(draws), dims[axis_at] // shards_of).reshape((-1,) + (1,) * (len(dims) - 1 - axis_at))
    return loudness


def centred(rng, dims, scale, limit, cuts=(), kind=jnp.bfloat16):
    factor_of = level_of(rng, dims, cuts, -0.22, 0.18) if cuts else 1.0
    values = jax.random.normal(rng, dims, jnp.float32) * scale * factor_of
    return jnp.minimum(jnp.maximum(values, -limit), limit).astype(kind)


def setup_inputs(seed: int = 0) -> dict:
    key_list = jax.random.split(jax.random.key(seed), 5)
    return {
        "picture_vectors": centred(key_list[0], (MATCHED_ROWS_NUM, D), 0.03, 0.2, ((0, 256),), jnp.float32),
        "caption_vectors": centred(key_list[1], (MATCHED_ROWS_NUM, D), 0.03, 0.2, ((0, 256),), jnp.float32),
        "warmth_exponent": jnp.clip(jax.random.uniform(key_list[2], (1,), jnp.float32, 3.0, 3.7), 3.0, 3.7),
        "offset_weight": jnp.clip(jax.random.uniform(key_list[3], (1,), jnp.float32, -8.0, -5.0), -8.0, -5.0),
    }


def unit_rows(values):
    row_norm = jnp.sqrt(lax.optimization_barrier(jnp.sum(values * values, axis=1, keepdims=True)) + 1e-06)
    return (values / row_norm, row_norm)

def project_back(unit, row_norm, grads):
    inner = lax.optimization_barrier(jnp.sum(unit * grads, axis=1, keepdims=True))
    return (grads - unit * inner) / row_norm

def reference(picture_vectors, caption_vectors, warmth_exponent, offset_weight):
    full_accuracy_mode = lax.Precision.HIGHEST
    image_unit, image_norm = unit_rows(picture_vectors)
    caption_unitlength, text_norm = unit_rows(caption_vectors)
    warmth_multiplier = jnp.exp(warmth_exponent[0])
    rotation_offset = offset_weight[0]
    block_size = math.gcd(MATCHED_ROWS_NUM, 512)
    block_count = MATCHED_ROWS_NUM // block_size
    columns = jnp.arange(MATCHED_ROWS_NUM, dtype=jnp.int32)

    def accumulate(state_now, block_index):
        caption_running_derivative, loss_acc, temp_acc, bias_acc = state_now
        start = (block_index * block_size).astype(jnp.int32)
        tile_span_rows = lax.dynamic_slice_in_dim(image_unit, start, block_size, 0)
        cosine_affinity_grid = jnp.dot(tile_span_rows, caption_unitlength.T, precision=full_accuracy_mode, preferred_element_type=jnp.float32)
        pairwise_energy_grid = warmth_multiplier * cosine_affinity_grid + rotation_offset
        row_ids = start + jnp.arange(block_size, dtype=jnp.int32)
        labels = jnp.where(row_ids[:, None] == columns[None, :], 1.0, -1.0).astype(cosine_affinity_grid.dtype)
        losses = jax.nn.softplus(-labels * pairwise_energy_grid)
        energy_derivative_grid = -labels * jax.nn.sigmoid(-labels * pairwise_energy_grid)
        picture_contract_spec = warmth_multiplier * jnp.dot(energy_derivative_grid, caption_unitlength, precision=full_accuracy_mode, preferred_element_type=jnp.float32)
        caption_running_derivative = caption_running_derivative + warmth_multiplier * jnp.dot(energy_derivative_grid.T, tile_span_rows, precision=full_accuracy_mode, preferred_element_type=jnp.float32)
        return ((caption_running_derivative, loss_acc + jnp.sum(losses), temp_acc + jnp.sum(energy_derivative_grid * cosine_affinity_grid), bias_acc + jnp.sum(energy_derivative_grid)), picture_contract_spec)
    start_state = (jnp.zeros((MATCHED_ROWS_NUM, D), jnp.float32), jnp.zeros((), jnp.float32), jnp.zeros((), jnp.float32), jnp.zeros((), jnp.float32))
    closing_carry, image_parts = lax.scan(accumulate, start_state, jnp.arange(block_count, dtype=jnp.int32))
    caption_contract_spec, penalty_accrued, warmth_accrued, offset_accrued = closing_carry
    picture_contract_spec = image_parts.reshape(MATCHED_ROWS_NUM, D)
    picture_derivative = project_back(image_unit, image_norm, picture_contract_spec)
    caption_derivative = project_back(caption_unitlength, text_norm, caption_contract_spec)
    mean_sigmoid_penalty = (penalty_accrued / MATCHED_ROWS_NUM).reshape(1)
    warmth_derivative = (warmth_multiplier * warmth_accrued / MATCHED_ROWS_NUM).reshape(1)
    offset_derivative = (offset_accrued / MATCHED_ROWS_NUM).reshape(1)
    return (mean_sigmoid_penalty, picture_derivative, caption_derivative, warmth_derivative, offset_derivative)
```

```python
import functools

import jax
import jax.numpy as jnp
from jax import lax
from jax.experimental import pallas as pl
from jax.experimental.pallas import tpu as pltpu
from jax.sharding import PartitionSpec as P

MESH = pl.DeviceIdType.MESH
F32, BF16 = jnp.float32, jnp.bfloat16
NX, NY, NZ = 4, 4, 8
SHARD, HALF, QUARTER, D = 64, 32, 16, 1152
ROWS = 1024
TI, TT = 256, 512
NT = (((1,), (1,)), ((), ()))
NN = (((1,), (0,)), ((), ()))
TN = (((0,), (0,)), ((), ()))


def dot(a, b, dims):
    return lax.dot_general(a, b, dims, preferred_element_type=F32)


def image_row(k, r):
    chunk, side = {0: (3, 0), 4: (3, 1), 1: (0, 0), 7: (0, 1), 2: (1, 0), 6: (1, 1), 3: (2, 0), 5: (2, 1)}[r]
    return chunk * 256 + side * 128 + k * 64


def text_row(h, p, q):
    if q == 0:
        at = h * 4 + p
    elif q == 2:
        at = 24 + h * 4 + p
    else:
        at = 8 + h * 8 + p * 2 + (q == 3)
    return at * HALF


def unit_rows(values):
    norm = jnp.sqrt(jnp.sum(values * values, axis=1, keepdims=True) + 1e-06)
    return values / norm, norm


def project_back(unit, norm, grads):
    inner = jnp.sum(unit * grads, axis=1, keepdims=True)
    return (grads - unit * inner) / norm


def pair_terms(scores, same, temperature, offset):
    logits = temperature * scores + offset
    e = jnp.exp(logits)
    u = 1.0 + e
    r = 1.0 / u
    slopes = jnp.where(same, -r, e * r)
    g = jnp.where(same, 1.0 / e, e)
    small = g * (1.0 - g * (0.5 - g * (1.0 / 3.0)))
    losses = jnp.where(g < 0.015625, small, jnp.log(1.0 + g))
    return losses, slopes


def kernel(pic, cap, warmth, bias, o_sum, o_pic, o_cap,
           img, txt, ih, il, th, tl, d_img, d_txt, s_ref, sh_ref, sl_ref, rid, cid, acc,
           got_s, got_z, got_t, sum_own, sum_z, sum_x, sum_y, sum_s,
           zs, zr, ss, sr, ts, tr, rzs, rzr, rss, rsr, rts, rtr, qs, qr):
    im = lax.axis_index("img")
    tx = lax.axis_index("txt")
    z, x = im // NX, im % NX
    y, c = tx // 2, tx % 2

    def at(dx=0, dy=0, dz=0, dc=0):
        return (((z + dz) % NZ) * NX + (x + dx) % NX, ((y + dy) % NY) * 2 + (c + dc) % 2)

    near = {"x+": at(dx=1), "x-": at(dx=3), "y+": at(dy=1), "y-": at(dy=3), "z+": at(dz=1), "z-": at(dz=7), "s": at(dc=1)}
    others = list(near.values()) + [at(dz=k) for k in (2, 3, 4, 5, 6)] + [at(dx=2), at(dy=2)]
    barrier = pltpu.get_barrier_semaphore()
    for other in others:
        pl.semaphore_signal(barrier, inc=1, device_id=other, device_id_type=MESH)

    pic_unit, pic_norm = unit_rows(pic[...])
    cap_unit, cap_norm = unit_rows(cap[...])
    own_i = image_row(0, 0)
    img[own_i:own_i + SHARD, :] = pic_unit
    for h in (0, 1):
        t0 = text_row(h, 0, 0)
        txt[t0:t0 + HALF, :] = cap_unit[h * HALF:(h + 1) * HALF, :]
    temperature = jnp.exp(warmth[0:1, 0:1])
    offset = bias[0:1, 0:1]

    for k in (0, 1):
        for r in range(NZ):
            block = (((z + NZ - r) % NZ) * NX + x) * (2 * NY) + y * 2 + (c + k) % 2
            base = image_row(k, r)
            rid[base:base + SHARD, :] = block * SHARD + lax.broadcasted_iota(jnp.int32, (SHARD, 128), 0)
    lane = lax.broadcasted_iota(jnp.int32, (8, 128), 1)
    for tile in range(ROWS // 128):
        ids = jnp.zeros((8, 128), jnp.int32)
        for h in (0, 1):
            for p in range(4):
                for q in range(4):
                    pos = text_row(h, p, q)
                    if pos // 128 == tile:
                        a, b = (p, q) if h == 0 else (q, p)
                        block = (((y + NY - b) % NY) * 2 + c) * (NX * NZ) + z * NX + (x + NX - a) % NX
                        off = pos % 128
                        inside = (lane >= off) & (lane < off + HALF)
                        ids = jnp.where(inside, block * SHARD + h * HALF + lane - off, ids)
        cid[:, tile * 128:(tile + 1) * 128] = ids

    pl.semaphore_wait(barrier, len(others))

    def remote(src, dst, s, r, dev):
        return pltpu.make_async_remote_copy(src_ref=src, dst_ref=dst, send_sem=s, recv_sem=r, device_id=dev, device_id_type=MESH)

    pending = []

    def go(copy):
        copy.start()
        pending.append(copy)

    def z_copy(s, d):
        src, dst = ((s - 1), s) if d == 0 else ((9 - s) % 8, 8 - s)
        off, n = (0, SHARD) if s < 4 else ((0, HALF) if d == 0 else (HALF, HALF))
        return remote(img.at[pl.ds(image_row(0, src) + off, n)], img.at[pl.ds(image_row(0, dst) + off, n)],
                      zs.at[s - 1, d], zr.at[s - 1, d], near["z+" if d == 0 else "z-"])

    def s_copy(r):
        return remote(img.at[pl.ds(image_row(0, r), SHARD)], img.at[pl.ds(image_row(1, r), SHARD)], ss.at[r], sr.at[r], near["s"])

    def t_index(h, phase, p, s, d):
        return h * 20 + (0 if phase == 0 else 4 + p * 4) + (s - 1) * 2 + d

    def t_copy(h, phase, p, s, d):
        src, dst = (s - 1, s) if d == 0 else ((5 - s) % 4, 4 - s)
        off, n = (0, HALF) if s < 2 else ((0, QUARTER) if d == 0 else (QUARTER, QUARTER))
        a, b = (text_row(h, src, 0), text_row(h, dst, 0)) if phase == 0 else (text_row(h, p, src), text_row(h, p, dst))
        i = t_index(h, phase, p, s, d)
        axis = ("xy", "yx")[h][phase]
        return remote(txt.at[pl.ds(a + off, n)], txt.at[pl.ds(b + off, n)], ts.at[i], tr.at[i], near[axis + ("+" if d == 0 else "-")])

    keys = [(h, 0, 0, s, d) for h in (0, 1) for s in (1, 2) for d in (0, 1)]
    keys += [(h, 1, p, s, d) for h in (0, 1) for p in range(4) for s in (1, 2) for d in (0, 1)]
    T = {k: t_copy(*k) for k in keys}
    Z = {(s, d): z_copy(s, d) for s in range(1, 5) for d in (0, 1)}
    S = {r: s_copy(r) for r in range(NZ)}
    HD = [(h, d) for d in (0, 1) for h in (0, 1)]

    for d in (0, 1):
        go(Z[1, d])
    for h, d in HD:
        go(T[h, 0, 0, 1, d])
    for h, d in HD:
        go(T[h, 1, 0, 1, d])
    go(S[0])
    for h, d in HD:
        T[h, 0, 0, 1, d].wait_recv()
        go(T[h, 0, 0, 2, d])
    for d in (0, 1):
        for h in (0, 1):
            for e in (0, 1):
                go(T[h, 1, 1 if d == 0 else 3, 1, e])
    for d in (0, 1):
        Z[1, d].wait_recv()
        go(Z[2, d])
    go(S[1])
    go(S[7])
    for h, d in HD:
        T[h, 0, 0, 2, d].wait_recv()
    for h in (0, 1):
        for e in (0, 1):
            go(T[h, 1, 2, 1, e])
    for h, d in HD:
        T[h, 1, 0, 1, d].wait_recv()
        go(T[h, 1, 0, 2, d])
    for d in (0, 1):
        Z[2, d].wait_recv()
        go(Z[3, d])
    go(S[2])
    go(S[6])
    for p in (1, 3):
        for h, d in HD:
            T[h, 1, p, 1, d].wait_recv()
            go(T[h, 1, p, 2, d])
    for d in (0, 1):
        Z[3, d].wait_recv()
        go(Z[4, d])
    go(S[3])
    go(S[5])
    for h, d in HD:
        T[h, 1, 2, 1, d].wait_recv()
        go(T[h, 1, 2, 2, d])
    for p in (0, 1, 3, 2):
        for h, d in HD:
            T[h, 1, p, 2, d].wait_recv()
    for d in (0, 1):
        Z[4, d].wait_recv()
    go(S[4])
    for r in range(NZ):
        S[r].wait_recv()
    for copy in pending:
        copy.wait_send()
    pending.clear()

    def split(i, _):
        rows = pl.ds(pl.multiple_of(i * 32, 32), 32)
        for src, hi, lo in ((img, ih, il), (txt, th, tl)):
            v = src[rows, :]
            top = v.astype(BF16)
            hi[rows, :] = top
            lo[rows, :] = (v - top.astype(F32)).astype(BF16)
        return 0

    lax.fori_loop(0, ROWS // 32, split, 0)
    d_txt[...] = jnp.zeros_like(d_txt)
    d_img[...] = jnp.zeros_like(d_img)
    acc[...] = jnp.zeros_like(acc)

    def tile(n, _):
        i, t = n // (ROWS // TT), n % (ROWS // TT)
        ri = pl.ds(pl.multiple_of(i * TI, TI), TI)
        rt = pl.ds(pl.multiple_of(t * TT, TT), TT)
        i_hi, i_lo, t_hi, t_lo = ih[ri, :], il[ri, :], th[rt, :], tl[rt, :]
        s_ref[...] = dot(jnp.concatenate([i_hi, i_lo, i_hi], 1), jnp.concatenate([t_hi, t_hi, t_lo], 1), NT)
        for b in range(TI // 32):
            scores = s_ref[b * 32:(b + 1) * 32, :]
            row = rid[pl.ds(pl.multiple_of(i * TI + b * 32, 32), 32), :]
            row = jnp.concatenate([row] * (TT // 128), 1)
            col = cid[:, rt]
            same = row == jnp.concatenate([col] * 4, 0)
            losses, slopes = pair_terms(scores, same, temperature, offset)
            for n_acc, v in enumerate((losses, slopes * scores, slopes)):
                acc[n_acc] += v[0:8] + v[8:16] + v[16:24] + v[24:32]
            hi = slopes.astype(BF16)
            sh_ref[b * 32:(b + 1) * 32, :] = hi
            sl_ref[b * 32:(b + 1) * 32, :] = (slopes - hi.astype(F32)).astype(BF16)
        sh, sl = sh_ref[...], sl_ref[...]
        d_img[ri, :] += dot(jnp.concatenate([sh, sl, sh], 1), jnp.concatenate([t_hi, t_hi, t_lo], 0), NN)
        d_txt[rt, :] += dot(jnp.concatenate([sh, sl, sh], 0), jnp.concatenate([i_hi, i_hi, i_lo], 0), TN)
        return 0

    lax.fori_loop(0, (ROWS // TI) * (ROWS // TT), tile, 0)

    for n_acc in range(3):
        v = acc[n_acc]
        v = v[:, 0:128] + v[:, 128:256] + v[:, 256:384] + v[:, 384:512]
        sum_own[0, n_acc:n_acc + 1, :] = jnp.sum(v, axis=0, keepdims=True)
    sum_own[0, 3:8, :] = jnp.zeros((5, 128), F32)

    def fan(stage, buf, size, base, where):
        copies = [remote(sum_own.at[stage], buf.at[k - 1], qs.at[base + k - 1], qr.at[base + k - 1], where(k)) for k in range(1, size)]
        for copy in copies:
            go(copy)
        return copies

    def fold(stage, buf, copies):
        total = sum_own[stage]
        for k, copy in enumerate(copies):
            copy.wait_recv()
            total = total + buf[k]
        sum_own[stage + 1] = total

    def rs_copy(r):
        return remote(d_img.at[pl.ds(image_row(1, r), SHARD)], got_s.at[r], rss.at[r], rsr.at[r], near["s"])

    def rz_copy(s, d):
        r = s if d == 0 else 8 - s
        off, n = (0, SHARD) if s < 4 else ((0, HALF) if d == 0 else (HALF, HALF))
        return remote(d_img.at[pl.ds(image_row(0, r) + off, n)], got_z.at[s - 1, d, pl.ds(0, n)],
                      rzs.at[s - 1, d], rzr.at[s - 1, d], near["z-" if d == 0 else "z+"])

    def rt_copy(h, phase, p, s, d):
        q = s if d == 0 else 4 - s
        off, n = (0, HALF) if s < 2 else ((0, QUARTER) if d == 0 else (QUARTER, QUARTER))
        a = text_row(h, q, 0) if phase == 0 else text_row(h, p, q)
        i = t_index(h, phase, p, s, d)
        axis = ("xy", "yx")[h][phase]
        return remote(d_txt.at[pl.ds(a + off, n)], got_t.at[i, pl.ds(0, n)], rts.at[i], rtr.at[i], near[axis + ("-" if d == 0 else "+")])

    RT = {k: rt_copy(*k) for k in keys}
    RZ = {(s, d): rz_copy(s, d) for s in range(1, 5) for d in (0, 1)}
    RS = {r: rs_copy(r) for r in range(NZ)}

    def add_t(h, phase, p, s, d):
        RT[h, phase, p, s, d].wait_recv()
        q = s - 1 if d == 0 else (5 - s) % 4
        off, n = (0, HALF) if s < 2 else ((0, QUARTER) if d == 0 else (QUARTER, QUARTER))
        a = (text_row(h, q, 0) if phase == 0 else text_row(h, p, q)) + off
        d_txt[a:a + n, :] += got_t[t_index(h, phase, p, s, d), 0:n, :]

    def add_z(s, d):
        RZ[s, d].wait_recv()
        r = s - 1 if d == 0 else (9 - s) % 8
        off, n = (0, SHARD) if s < 4 else ((0, HALF) if d == 0 else (HALF, HALF))
        a = image_row(0, r) + off
        d_img[a:a + n, :] += got_z[s - 1, d, 0:n, :]

    def add_s(r):
        RS[r].wait_recv()
        a = image_row(0, r)
        d_img[a:a + SHARD, :] += got_s[r]

    for r in (4, 3, 5, 2, 6, 1, 7, 0):
        go(RS[r])
    for p in (2, 1, 3, 0):
        for h, d in HD:
            go(RT[h, 1, p, 2, d])
    add_s(4)
    for d in (0, 1):
        go(RZ[4, d])
    z_sums = fan(0, sum_z, NZ, 0, lambda k: at(dz=k))
    for r in (3, 5, 2, 6, 1, 7, 0):
        add_s(r)
    for p in (2, 1, 3):
        for h, d in HD:
            add_t(h, 1, p, 2, d)
            go(RT[h, 1, p, 1, d])
        if p == 2:
            for d in (0, 1):
                add_z(4, d)
                go(RZ[3, d])
            fold(0, sum_z, z_sums)
            x_sums = fan(1, sum_x, NX, 7, lambda k: at(dx=k))
    for h, d in HD:
        add_t(h, 1, 0, 2, d)
        go(RT[h, 1, 0, 1, d])
    for d in (0, 1):
        add_z(3, d)
        go(RZ[2, d])
    fold(1, sum_x, x_sums)
    y_sums = fan(2, sum_y, NY, 10, lambda k: at(dy=k))
    for h, d in HD:
        add_t(h, 1, 2, 1, d)
    for h, d in HD:
        go(RT[h, 0, 0, 2, d])
    for d in (0, 1):
        add_z(2, d)
        go(RZ[1, d])
    fold(2, sum_y, y_sums)
    s_sums = fan(3, sum_s, 2, 13, lambda k: at(dc=1))
    for p in (1, 3):
        for h, d in HD:
            add_t(h, 1, p, 1, d)
    for h, d in HD:
        add_t(h, 0, 0, 2, d)
        go(RT[h, 0, 0, 1, d])
    for h, d in HD:
        add_t(h, 1, 0, 1, d)
    for d in (0, 1):
        add_z(1, d)
    o_pic[...] = project_back(pic_unit, pic_norm, temperature * d_img[own_i:own_i + SHARD, :])
    fold(3, sum_s, s_sums)
    totals = jnp.sum(sum_own[4], axis=1, keepdims=True) * (1.0 / 16384.0)
    kind = lax.broadcasted_iota(jnp.int32, (8, 1), 0)
    o_sum[...] = jnp.broadcast_to(jnp.where(kind == 1, temperature * totals, totals), (8, 128))
    for h, d in HD:
        add_t(h, 0, 0, 1, d)
    grads = jnp.concatenate([d_txt[text_row(h, 0, 0):text_row(h, 0, 0) + HALF, :] for h in (0, 1)], 0)
    o_cap[...] = project_back(cap_unit, cap_norm, temperature * grads)
    for copy in pending:
        copy.wait_send()


def body(picture_vectors, caption_vectors, warmth_exponent, offset_weight):
    vmem = pl.BlockSpec(memory_space=pltpu.VMEM)
    dma = pltpu.SemaphoreType.DMA
    big, split = pltpu.VMEM((ROWS, D), F32), pltpu.VMEM((ROWS, D), BF16)
    sums, picture_derivative, caption_derivative = pl.pallas_call(
        kernel,
        out_shape=[jax.ShapeDtypeStruct((8, 128), F32), jax.ShapeDtypeStruct((SHARD, D), F32), jax.ShapeDtypeStruct((SHARD, D), F32)],
        in_specs=[vmem] * 4,
        out_specs=[vmem] * 3,
        scratch_shapes=[
            big, big, split, split, split, split, big, big,
            pltpu.VMEM((TI, TT), F32), pltpu.VMEM((TI, TT), BF16), pltpu.VMEM((TI, TT), BF16),
            pltpu.VMEM((ROWS, 128), jnp.int32), pltpu.VMEM((8, ROWS), jnp.int32), pltpu.VMEM((3, 8, TT), F32),
            pltpu.VMEM((NZ, SHARD, D), F32), pltpu.VMEM((4, 2, SHARD, D), F32), pltpu.VMEM((40, HALF, D), F32),
            pltpu.VMEM((5, 8, 128), F32), pltpu.VMEM((7, 8, 128), F32), pltpu.VMEM((3, 8, 128), F32),
            pltpu.VMEM((3, 8, 128), F32), pltpu.VMEM((1, 8, 128), F32),
            dma((4, 2)), dma((4, 2)), dma((NZ,)), dma((NZ,)), dma((40,)), dma((40,)),
            dma((4, 2)), dma((4, 2)), dma((NZ,)), dma((NZ,)), dma((40,)), dma((40,)), dma((14,)), dma((14,)),
        ],
        compiler_params=pltpu.CompilerParams(collective_id=0, has_side_effects=True, vmem_limit_bytes=60 * 2**20),
    )(
        picture_vectors,
        caption_vectors,
        jnp.broadcast_to(warmth_exponent.reshape(1, 1), (8, 128)),
        jnp.broadcast_to(offset_weight.reshape(1, 1), (8, 128)),
    )
    return sums[0, 0:1], picture_derivative, caption_derivative, sums[1, 0:1], sums[2, 0:1]


def solution(mesh):
    in_specs = (P(("img", "txt"), None), P(("txt", "img"), None), P(), P())
    out_specs = (P(), P(("img", "txt"), None), P(("txt", "img"), None), P(), P())
    return jax.shard_map(body, mesh=mesh, in_specs=in_specs, out_specs=out_specs, check_vma=False)
```

```python
import functools

import jax
import jax.numpy as jnp
from jax import lax
from jax.experimental import pallas as pl
from jax.experimental.pallas import tpu as pltpu
from jax.sharding import PartitionSpec as P

MESH = pl.DeviceIdType.MESH
F32, BF16, F8 = jnp.float32, jnp.bfloat16, jnp.float8_e4m3fn
UP = 4096.0
NX, NY, NZ = 4, 4, 8
SHARD, HALF, QUARTER, D = 64, 32, 16, 1152
ROWS = 1024
SHARE = {0: 0, 1: 1, 7: 1, 2: 2, 6: 2, 3: 3, 5: 3, 4: 3}
BACK = {4: 0, 3: 1, 5: 1, 2: 2, 6: 2, 1: 2, 7: 2, 0: 2}
NT = (((1,), (1,)), ((), ()))
NN = (((1,), (0,)), ((), ()))
TN = (((0,), (0,)), ((), ()))


def dot(a, b, dims):
    return lax.dot_general(a, b, dims, preferred_element_type=F32)


def image_row(k, r):
    return {0: 0, 1: 128, 7: 256, 2: 384, 6: 512, 3: 640, 5: 768, 4: 896}[r] + k * SHARD


def text_row(h, p, q):
    if q == 0:
        at = h * 4 + p
    elif q == 2:
        at = 24 + h * 4 + p
    else:
        at = 8 + h * 8 + p * 2 + (q == 3)
    return at * HALF


def unit_rows(values):
    norm = jnp.sqrt(jnp.sum(values * values, axis=1, keepdims=True) + 1e-06)
    return values / norm, norm


def project_back(unit, norm, grads):
    inner = jnp.sum(unit * grads, axis=1, keepdims=True)
    return (grads - unit * inner) / norm


def pair_terms(scores, same, temperature, offset):
    logits = temperature * scores + offset
    e = jnp.exp(logits)
    u = 1.0 + e
    r = 1.0 / u
    slopes = jnp.where(same, -r, e * r)
    g = jnp.where(same, 1.0 / e, e)
    small = g * (1.0 - g * (0.5 - g * (1.0 / 3.0)))
    losses = jnp.where(g < 0.015625, small, jnp.log(1.0 + g))
    return losses, slopes


def kernel(pic, cap, warmth, bias, o_sum, o_pic, o_cap,
           img, txt, ih, il, th, tl, ih8, il8, th8, tl8, d_img, d_txt, s_ref, sh_ref, sh8_ref, sl8_ref, rid, cid, acc,
           got_s, got_z, got_t, sum_own, sum_got, zr, sr, tr, rzr, rsr, rtr, qr, sent):
    im = lax.axis_index("img")
    tx = lax.axis_index("txt")
    z, x = im // NX, im % NX
    y, c = tx // 2, tx % 2

    def at(dx=0, dy=0, dz=0, dc=0):
        return (((z + dz) % NZ) * NX + (x + dx) % NX, ((y + dy) % NY) * 2 + (c + dc) % 2)

    near = {"x+": at(dx=1), "x-": at(dx=3), "y+": at(dy=1), "y-": at(dy=3), "z+": at(dz=1), "z-": at(dz=7), "s": at(dc=1)}
    others = list(near.values()) + [at(dz=k) for k in (2, 3, 4, 5, 6)] + [at(dx=2), at(dy=2)]
    barrier = pltpu.get_barrier_semaphore()
    for other in others:
        pl.semaphore_signal(barrier, inc=1, device_id=other, device_id_type=MESH)

    pic_unit, pic_norm = unit_rows(pic[...])
    cap_unit, cap_norm = unit_rows(cap[...])
    own_i = image_row(0, 0)
    img[own_i:own_i + SHARD, :] = pic_unit
    for h in (0, 1):
        t0 = text_row(h, 0, 0)
        txt[t0:t0 + HALF, :] = cap_unit[h * HALF:(h + 1) * HALF, :]
    temperature = jnp.exp(jnp.full((1, 1), warmth[0], F32))
    offset = jnp.full((1, 1), bias[0], F32)
    warm_down = temperature * (1.0 / (UP * UP))

    pl.semaphore_wait(barrier, len(others))

    def remote(src, dst, s, r, dev):
        return pltpu.make_async_remote_copy(src_ref=src, dst_ref=dst, send_sem=s, recv_sem=r, device_id=dev, device_id_type=MESH)

    def landed(rows, sem):
        pltpu.make_async_copy(d_img.at[pl.ds(0, rows)], d_img.at[pl.ds(0, rows)], sem).wait()

    def go(copy):
        copy.start()

    def z_group(s, d, h):
        return (s - 1) * 2 + ((h if d == 0 else 1 - h) if s < 4 else 0)

    def t_group(phase, p, s):
        return (0 if phase == 0 else 2 + 2 * p) + s - 1

    def z_copy(s, d, h):
        src, dst = ((s - 1), s) if d == 0 else ((9 - s) % 8, 8 - s)
        return remote(img.at[pl.ds(image_row(0, src) + h * HALF, HALF)], img.at[pl.ds(image_row(0, dst) + h * HALF, HALF)],
                      sent.at[0], zr.at[z_group(s, d, h)], near["z+" if d == 0 else "z-"])

    def s_copy(r):
        return remote(img.at[pl.ds(image_row(0, r), SHARD)], img.at[pl.ds(image_row(1, r), SHARD)], sent.at[1], sr.at[SHARE[r]], near["s"])

    def t_index(h, phase, p, s, d):
        return h * 20 + (0 if phase == 0 else 4 + p * 4) + (s - 1) * 2 + d

    def t_copy(h, phase, p, s, d):
        src, dst = (s - 1, s) if d == 0 else ((5 - s) % 4, 4 - s)
        off, n = (0, HALF) if s < 2 else ((0, QUARTER) if d == 0 else (QUARTER, QUARTER))
        a, b = (text_row(h, src, 0), text_row(h, dst, 0)) if phase == 0 else (text_row(h, p, src), text_row(h, p, dst))
        axis = ("xy", "yx")[h][phase]
        return remote(txt.at[pl.ds(a + off, n)], txt.at[pl.ds(b + off, n)], sent.at[2], tr.at[t_group(phase, p, s)], near[axis + ("+" if d == 0 else "-")])

    keys = [(h, 0, 0, s, d) for h in (0, 1) for s in (1, 2) for d in (0, 1)]
    keys += [(h, 1, p, s, d) for h in (0, 1) for p in range(4) for s in (1, 2) for d in (0, 1)]
    z_keys = [(s, d, h) for s in (1, 2, 3) for d in (0, 1) for h in (0, 1)] + [(4, 0, 0), (4, 1, 1)]
    T = {k: t_copy(*k) for k in keys}
    Z = {k: z_copy(*k) for k in z_keys}
    S = {r: s_copy(r) for r in range(NZ)}
    HD = [(h, d) for d in (0, 1) for h in (0, 1)]

    def pass_z(s, n):
        landed(2 * HALF, zr.at[z_group(s, 0, n)])
        for d in (0, 1):
            h = n if d == 0 else 1 - n
            if (s + 1, d, h) in Z:
                go(Z[s + 1, d, h])

    def pass_t(phase, p, s):
        landed(4 * HALF if s == 1 else 4 * QUARTER, tr.at[t_group(phase, p, s)])
        for h, d in HD:
            if s == 1:
                go(T[h, phase, p, 2, d])

    def share(*rs):
        for r in rs:
            go(S[r])

    def split(src, hi, lo, hi8, lo8, first, last):
        def step(i, _):
            rows = pl.ds(pl.multiple_of(first + i * 32, 32), 32)
            v = src[rows, :] * UP
            top = v.astype(BF16)
            rest = v - top.astype(F32)
            hi[rows, :] = top
            lo[rows, :] = rest.astype(BF16)
            hi8[rows, :] = (v * 0.0625).astype(F8)
            lo8[rows, :] = (rest * 16.0).astype(F8)
            return 0

        lax.fori_loop(0, (last - first) // 32, step, 0)

    def split_i(first, last):
        split(img, ih, il, ih8, il8, first, last)

    def split_t(first, last):
        split(txt, th, tl, th8, tl8, first, last)

    def block(i0, i1, t0, t1, first_i, first_t):
        ri, rt = slice(i0, i1), slice(t0, t1)
        ni, nt = i1 - i0, t1 - t0
        i_hi, i_lo, t_hi, t_lo = ih[ri, :], il[ri, :], th[rt, :], tl[rt, :]
        s_ref[ri, rt] = dot(jnp.concatenate([i_hi, i_lo, i_hi], 1), jnp.concatenate([t_hi, t_hi, t_lo], 1), NT)
        n = max(8192 // nt // 32, 1) * 32
        sums = [jnp.zeros((8, nt), F32)] * 3
        for b in range(i0, i1, n):
            rows = slice(b, b + n)
            scores = s_ref[rows, rt]
            row = jnp.concatenate([rid[rows, :]] * (nt // 128), 1)
            same = row == jnp.concatenate([cid[:, rt]] * (n // 8), 0)
            losses, slopes = pair_terms(scores, same, warm_down, offset)
            sums = [a + jnp.sum(v.reshape(n // 8, 8, nt), axis=0) for a, v in zip(sums, (losses, slopes * scores, slopes))]
            slopes = slopes * UP
            hi = slopes.astype(BF16)
            sh_ref[rows, rt] = hi
            sh8_ref[rows, rt] = (slopes * 0.0625).astype(F8)
            sl8_ref[rows, rt] = ((slopes - hi.astype(F32)) * 16.0).astype(F8)
        for k, v in enumerate(sums):
            acc[k] += sum(v[:, q:q + 128] for q in range(0, nt, 128))
        sh, sh8, sl8 = sh_ref[ri, rt], sh8_ref[ri, rt], sl8_ref[ri, rt]
        g = dot(sh, t_hi, NN) + dot(jnp.concatenate([sl8, sh8], 1), jnp.concatenate([th8[rt, :], tl8[rt, :]], 0), NN)
        d_img[ri, :] = g if first_i else d_img[ri, :] + g
        g = dot(sh, i_hi, TN) + dot(jnp.concatenate([sl8, sh8], 0), jnp.concatenate([ih8[ri, :], il8[ri, :]], 0), TN)
        d_txt[rt, :] = g if first_t else d_txt[rt, :] + g

    for n in (0, 1):
        for d in (0, 1):
            go(Z[1, d, n if d == 0 else 1 - n])
    for h, d in HD:
        go(T[h, 0, 0, 1, d])
    for h, d in HD:
        go(T[h, 1, 0, 1, d])
    share(0)

    for k in (0, 1):
        for r in range(NZ):
            number = (((z + NZ - r) % NZ) * NX + x) * (2 * NY) + y * 2 + (c + k) % 2
            base = image_row(k, r)
            rid[base:base + SHARD, :] = number * SHARD + lax.broadcasted_iota(jnp.int32, (SHARD, 128), 0)
    lane = lax.broadcasted_iota(jnp.int32, (8, 128), 1)
    for part in range(ROWS // 128):
        ids = jnp.zeros((8, 128), jnp.int32)
        for h in (0, 1):
            for p in range(4):
                for q in range(4):
                    pos = text_row(h, p, q)
                    if pos // 128 == part:
                        a, b = (p, q) if h == 0 else (q, p)
                        number = (((y + NY - b) % NY) * 2 + c) * (NX * NZ) + z * NX + (x + NX - a) % NX
                        off = pos % 128
                        inside = (lane >= off) & (lane < off + HALF)
                        ids = jnp.where(inside, number * SHARD + h * HALF + lane - off, ids)
        cid[:, part * 128:(part + 1) * 128] = ids
    acc[...] = jnp.zeros_like(acc)

    pass_t(0, 0, 1)
    for p in (1, 3):
        for h in (0, 1):
            for d in (0, 1):
                go(T[h, 1, p, 1, d])
    pass_z(1, 0)
    landed(SHARD, sr.at[0])
    split_i(0, 128)
    pass_z(1, 1)
    share(1, 7)
    pass_t(0, 0, 2)
    for h in (0, 1):
        for d in (0, 1):
            go(T[h, 1, 2, 1, d])
    split_t(0, 256)
    pass_z(2, 0)
    landed(2 * SHARD, sr.at[1])
    split_i(128, 384)
    block(0, 384, 0, 256, True, True)
    pass_t(1, 0, 1)
    pass_z(2, 1)
    share(2, 6)
    pass_t(1, 1, 1)
    landed(2 * SHARD, sr.at[2])
    split_i(384, 640)
    pass_t(1, 3, 1)
    pass_z(3, 0)
    block(384, 640, 0, 256, True, False)
    pass_t(1, 2, 1)
    split_t(256, 768)
    pass_z(3, 1)
    share(3, 5)
    block(0, 384, 256, 768, False, True)
    landed(2 * HALF, zr.at[6])
    share(4)
    block(384, 640, 256, 768, False, False)
    for p in (0, 1, 3, 2):
        pass_t(1, p, 2)
    split_t(768, 1024)
    landed(3 * SHARD, sr.at[3])
    split_i(640, 1024)
    for k, rows in enumerate((14 * HALF, NZ * SHARD, 15 * SHARD)):
        landed(rows, sent.at[k])

    def rs_copy(r):
        return remote(d_img.at[pl.ds(image_row(1, r), SHARD)], got_s.at[r], sent.at[1], rsr.at[BACK[r]], near["s"])

    def rz_copy(s, d, h):
        r = s if d == 0 else 8 - s
        return remote(d_img.at[pl.ds(image_row(0, r) + h * HALF, HALF)], got_z.at[s - 1, d, pl.ds(h * HALF, HALF)],
                      sent.at[0], rzr.at[z_group(s, 1 - d, h)], near["z-" if d == 0 else "z+"])

    def rt_copy(h, phase, p, s, d):
        q = s if d == 0 else 4 - s
        off, n = (0, HALF) if s < 2 else ((0, QUARTER) if d == 0 else (QUARTER, QUARTER))
        a = text_row(h, q, 0) if phase == 0 else text_row(h, p, q)
        i = t_index(h, phase, p, s, d)
        axis = ("xy", "yx")[h][phase]
        return remote(d_txt.at[pl.ds(a + off, n)], got_t.at[i, pl.ds(0, n)], sent.at[2], rtr.at[t_group(phase, p, s)], near[axis + ("-" if d == 0 else "+")])

    RT = {k: rt_copy(*k) for k in keys}
    RZ = {k: rz_copy(*k) for k in z_keys}
    RS = {r: rs_copy(r) for r in range(NZ)}

    def add_t(h, phase, p, s, d):
        q = s - 1 if d == 0 else (5 - s) % 4
        off, n = (0, HALF) if s < 2 else ((0, QUARTER) if d == 0 else (QUARTER, QUARTER))
        a = (text_row(h, q, 0) if phase == 0 else text_row(h, p, q)) + off
        d_txt[a:a + n, :] += got_t[t_index(h, phase, p, s, d), 0:n, :]

    def add_z(s, d, h):
        r = s - 1 if d == 0 else (9 - s) % 8
        a = image_row(0, r) + h * HALF
        d_img[a:a + HALF, :] += got_z[s - 1, d, h * HALF:(h + 1) * HALF, :]

    def add_s(r):
        a = image_row(0, r)
        d_img[a:a + SHARD, :] += got_s[r]

    def back_t(phase, p, s, then=None):
        landed(4 * HALF if s == 1 else 4 * QUARTER, rtr.at[t_group(phase, p, s)])
        for h, d in HD:
            add_t(h, phase, p, s, d)
            if then is not None:
                go(RT[(h,) + then + (d,)])

    def back_z(s, n):
        landed(2 * HALF, rzr.at[z_group(s, 0, n)])
        for d in (0, 1):
            h = (1 - n if d == 0 else n) if s < 4 else d
            add_z(s, d, h)
            if s > 1:
                go(RZ[s - 1, d, h])

    STAGES = ((0, NZ, lambda k: at(dz=k)), (7, NX, lambda k: at(dx=k)), (10, NY, lambda k: at(dy=k)), (13, 2, lambda k: at(dc=k)))

    def fan(stage):
        base, size, where = STAGES[stage]
        for k in range(1, size):
            go(remote(sum_own.at[stage], sum_got.at[base + k - 1], sent.at[3], qr.at[stage], where(k)))

    def fold(stage):
        base, size, _ = STAGES[stage]
        got = sum_got.at[pl.ds(base, size - 1)]
        pltpu.make_async_copy(got, got, qr.at[stage]).wait()
        total = sum_own[stage]
        for k in range(base, base + size - 1):
            total = total + sum_got[k]
        sum_own[stage + 1] = total

    block(0, 512, 768, 1024, False, True)
    block(512, 640, 768, 1024, False, False)
    block(640, 1024, 768, 1024, True, False)
    for p in (2, 1, 3, 0):
        for h, d in HD:
            go(RT[h, 1, p, 2, d])
    block(896, 1024, 0, 768, False, False)
    go(RS[4])
    block(640, 896, 0, 256, False, False)
    landed(SHARD, rsr.at[0])
    add_s(4)
    for d in (0, 1):
        go(RZ[4, d, d])
    block(640, 896, 256, 768, False, False)
    for r in (3, 5, 2, 6, 1, 7, 0):
        go(RS[r])
    for k in range(3):
        sum_own[0, k:k + 1, :] = jnp.sum(acc[k], axis=0, keepdims=True)
    sum_own[0, 3:8, :] = jnp.zeros((5, 128), F32)
    fan(0)
    back_t(1, 2, 2, (1, 2, 1))
    landed(2 * SHARD, rsr.at[1])
    for r in (3, 5):
        add_s(r)
    for d in (0, 1):
        go(RZ[3, d, 1 - d])
    back_z(4, 0)
    for p in (1, 3, 0):
        back_t(1, p, 2, (1, p, 1))
    landed(5 * SHARD, rsr.at[2])
    for r in (2, 6, 1, 7, 0):
        add_s(r)
    fold(0)
    fan(1)
    back_z(3, 0)
    back_t(1, 2, 1)
    for h, d in HD:
        go(RT[h, 0, 0, 2, d])
    back_z(3, 1)
    fold(1)
    fan(2)
    back_t(1, 1, 1)
    back_z(2, 0)
    back_t(1, 3, 1)
    back_t(0, 0, 2, (0, 0, 1))
    back_z(2, 1)
    fold(2)
    fan(3)
    back_z(1, 0)
    back_t(1, 0, 1)
    back_z(1, 1)
    o_pic[...] = project_back(pic_unit, pic_norm, warm_down * d_img[own_i:own_i + SHARD, :])
    fold(3)
    totals = jnp.sum(sum_own[4], axis=1, keepdims=True) * (1.0 / 16384.0)
    kind = lax.broadcasted_iota(jnp.int32, (8, 1), 0)
    o_sum[...] = jnp.broadcast_to(jnp.where(kind == 1, warm_down * totals, totals), (8, 128))
    back_t(0, 0, 1)
    grads = jnp.concatenate([d_txt[text_row(h, 0, 0):text_row(h, 0, 0) + HALF, :] for h in (0, 1)], 0)
    o_cap[...] = project_back(cap_unit, cap_norm, warm_down * grads)
    for k, rows in enumerate((14 * HALF, NZ * SHARD, 15 * SHARD)):
        landed(rows, sent.at[k])
    pltpu.make_async_copy(sum_got, sum_got, sent.at[3]).wait()


def finish(sums, pic, cap, o_loss, o_pic, o_cap, o_warmth, o_bias):
    o_loss[...] = sums[0:1, 0:1]
    o_warmth[...] = sums[1:2, 0:1]
    o_bias[...] = sums[2:3, 0:1]
    o_pic[...] = pic[...]
    o_cap[...] = cap[...]


def body(picture_vectors, caption_vectors, warmth_exponent, offset_weight):
    vmem, smem = pl.BlockSpec(memory_space=pltpu.VMEM), pl.BlockSpec(memory_space=pltpu.SMEM)
    dma = pltpu.SemaphoreType.DMA
    big, split, eighth = pltpu.VMEM((ROWS, D), F32), pltpu.VMEM((ROWS, D), BF16), pltpu.VMEM((ROWS, D), F8)
    one, shard = jax.ShapeDtypeStruct((1, 1), F32), jax.ShapeDtypeStruct((SHARD, D), F32)
    results = pl.pallas_call(
        kernel,
        out_shape=[jax.ShapeDtypeStruct((8, 128), F32), shard, shard],
        in_specs=[vmem, vmem, smem, smem],
        out_specs=[vmem] * 3,
        scratch_shapes=[
            big, big, split, split, split, split, eighth, eighth, eighth, eighth, big, big,
            pltpu.VMEM((ROWS, ROWS), F32), pltpu.VMEM((ROWS, ROWS), BF16), pltpu.VMEM((ROWS, ROWS), F8), pltpu.VMEM((ROWS, ROWS), F8),
            pltpu.VMEM((ROWS, 128), jnp.int32), pltpu.VMEM((8, ROWS), jnp.int32), pltpu.VMEM((3, 8, 128), F32),
            pltpu.VMEM((NZ, SHARD, D), F32), pltpu.VMEM((4, 2, SHARD, D), F32), pltpu.VMEM((40, HALF, D), F32),
            pltpu.VMEM((5, 8, 128), F32), pltpu.VMEM((14, 8, 128), F32),
            dma((7,)), dma((4,)), dma((10,)), dma((7,)), dma((3,)), dma((10,)), dma((4,)), dma((4,)),
        ],
        compiler_params=pltpu.CompilerParams(collective_id=0, has_side_effects=True, vmem_limit_bytes=62 * 2**20),
    )(picture_vectors, caption_vectors, warmth_exponent, offset_weight)
    loss, picture_derivative, caption_derivative, warmth, bias = pl.pallas_call(
        finish, out_shape=[one, shard, shard, one, one], in_specs=[vmem] * 3, out_specs=[vmem] * 5
    )(*results)
    return loss.reshape(1), picture_derivative, caption_derivative, warmth.reshape(1), bias.reshape(1)


def solution(mesh):
    in_specs = (P(("img", "txt"), None), P(("txt", "img"), None), P(), P())
    out_specs = (P(), P(("img", "txt"), None), P(("txt", "img"), None), P(), P())
    return jax.shard_map(body, mesh=mesh, in_specs=in_specs, out_specs=out_specs, check_vma=False)
```

```python
import functools

import jax
import jax.numpy as jnp
from jax import lax
from jax.experimental import pallas as pl
from jax.experimental.pallas import tpu as pltpu
from jax.sharding import PartitionSpec as P

MESH = pl.DeviceIdType.MESH
F32, BF16, F8 = jnp.float32, jnp.bfloat16, jnp.float8_e4m3fn
UP = 4096.0
NX, NY, NZ = 4, 4, 8
SHARD, HALF, QUARTER, D = 64, 32, 16, 1152
ROWS = 1024
SHARE = {0: 0, 1: 1, 7: 1, 2: 2, 6: 2, 3: 3, 5: 3, 4: 3}
BACK = {4: 0, 3: 1, 5: 1, 2: 2, 6: 2, 1: 2, 7: 2, 0: 2}
NT = (((1,), (1,)), ((), ()))
NN = (((1,), (0,)), ((), ()))
TN = (((0,), (0,)), ((), ()))


def dot(a, b, dims):
    return lax.dot_general(a, b, dims, preferred_element_type=F32)


def image_row(k, r):
    return {0: 0, 1: 128, 7: 256, 2: 384, 6: 512, 3: 640, 5: 768, 4: 896}[r] + k * SHARD


def text_row(h, p, q):
    if q == 0:
        at = h * 4 + p
    elif q == 2:
        at = 24 + h * 4 + p
    else:
        at = 8 + (0, 1, 3, 2)[p] * 4 + h * 2 + (q == 3)
    return at * HALF


def unit_rows(values):
    norm = jnp.sqrt(jnp.sum(values * values, axis=1, keepdims=True) + 1e-06)
    return values / norm, norm


def project_back(unit, norm, grads):
    inner = jnp.sum(unit * grads, axis=1, keepdims=True)
    return (grads - unit * inner) / norm


def pair_terms(scores, same, temperature, offset):
    logits = temperature * scores + offset
    e = jnp.exp(logits)
    u = 1.0 + e
    r = 1.0 / u
    slopes = jnp.where(same, -r, e * r)
    g = jnp.where(same, 1.0 / e, e)
    small = g * (1.0 - g * (0.5 - g * (1.0 / 3.0)))
    losses = jnp.where(g < 0.015625, small, jnp.log(1.0 + g))
    return losses, slopes


def kernel(pic, cap, warmth, bias, o_sum, o_pic, o_cap,
           img, txt, ih, il, th, tl, ih8, il8, th8, tl8, d_img, d_txt, s_ref, sh_ref, sh8_ref, sl8_ref, rid_i, cid_i, rid_t, cid_t, acc,
           got_s, got_z, got_t, sum_own, sum_got, zr, sr, tr, rzr, rsr, rtr, qr, sent):
    im = lax.axis_index("img")
    tx = lax.axis_index("txt")
    z, x = im // NX, im % NX
    y, c = tx // 2, tx % 2

    def at(dx=0, dy=0, dz=0, dc=0):
        return (((z + dz) % NZ) * NX + (x + dx) % NX, ((y + dy) % NY) * 2 + (c + dc) % 2)

    near = {"x+": at(dx=1), "x-": at(dx=3), "y+": at(dy=1), "y-": at(dy=3), "z+": at(dz=1), "z-": at(dz=7), "s": at(dc=1)}
    others = list(near.values()) + [at(dz=k) for k in (2, 3, 4, 5, 6)] + [at(dx=2), at(dy=2)]
    barrier = pltpu.get_barrier_semaphore()
    for other in others:
        pl.semaphore_signal(barrier, inc=1, device_id=other, device_id_type=MESH)

    pic_unit, pic_norm = unit_rows(pic[...])
    cap_unit, cap_norm = unit_rows(cap[...])
    own_i = image_row(0, 0)
    img[own_i:own_i + SHARD, :] = pic_unit
    for h in (0, 1):
        t0 = text_row(h, 0, 0)
        txt[t0:t0 + HALF, :] = cap_unit[h * HALF:(h + 1) * HALF, :]
    temperature = jnp.exp(jnp.full((1, 1), warmth[0], F32))
    offset = jnp.full((1, 1), bias[0], F32)
    warm_down = temperature * (1.0 / (UP * UP))

    pl.semaphore_wait(barrier, len(others))

    def remote(src, dst, s, r, dev):
        return pltpu.make_async_remote_copy(src_ref=src, dst_ref=dst, send_sem=s, recv_sem=r, device_id=dev, device_id_type=MESH)

    def landed(rows, sem):
        pltpu.make_async_copy(d_img.at[pl.ds(0, rows)], d_img.at[pl.ds(0, rows)], sem).wait()

    def go(copy):
        copy.start()

    def z_group(s, d, h):
        return (s - 1) * 2 + ((h if d == 0 else 1 - h) if s < 4 else 0)

    def t_group(phase, p, s):
        return (0 if phase == 0 else 2 + 2 * p) + s - 1

    def z_copy(s, d, h):
        src, dst = ((s - 1), s) if d == 0 else ((9 - s) % 8, 8 - s)
        return remote(img.at[pl.ds(image_row(0, src) + h * HALF, HALF)], img.at[pl.ds(image_row(0, dst) + h * HALF, HALF)],
                      sent.at[0], zr.at[z_group(s, d, h)], near["z+" if d == 0 else "z-"])

    def s_copy(r):
        return remote(img.at[pl.ds(image_row(0, r), SHARD)], img.at[pl.ds(image_row(1, r), SHARD)], sent.at[1], sr.at[SHARE[r]], near["s"])

    def t_index(h, phase, p, s, d):
        return h * 20 + (0 if phase == 0 else 4 + p * 4) + (s - 1) * 2 + d

    def t_copy(h, phase, p, s, d):
        src, dst = (s - 1, s) if d == 0 else ((5 - s) % 4, 4 - s)
        off, n = (0, HALF) if s < 2 else ((0, QUARTER) if d == 0 else (QUARTER, QUARTER))
        a, b = (text_row(h, src, 0), text_row(h, dst, 0)) if phase == 0 else (text_row(h, p, src), text_row(h, p, dst))
        axis = ("xy", "yx")[h][phase]
        return remote(txt.at[pl.ds(a + off, n)], txt.at[pl.ds(b + off, n)], sent.at[2], tr.at[t_group(phase, p, s)], near[axis + ("+" if d == 0 else "-")])

    keys = [(h, 0, 0, s, d) for h in (0, 1) for s in (1, 2) for d in (0, 1)]
    keys += [(h, 1, p, s, d) for h in (0, 1) for p in range(4) for s in (1, 2) for d in (0, 1)]
    z_keys = [(s, d, h) for s in (1, 2, 3) for d in (0, 1) for h in (0, 1)] + [(4, 0, 0), (4, 1, 1)]
    T = {k: t_copy(*k) for k in keys}
    Z = {k: z_copy(*k) for k in z_keys}
    S = {r: s_copy(r) for r in range(NZ)}
    HD = [(h, d) for d in (0, 1) for h in (0, 1)]

    def pass_z(s, n):
        landed(2 * HALF, zr.at[z_group(s, 0, n)])
        for d in (0, 1):
            h = n if d == 0 else 1 - n
            if (s + 1, d, h) in Z:
                go(Z[s + 1, d, h])

    def pass_t(phase, p, s):
        landed(4 * HALF if s == 1 else 4 * QUARTER, tr.at[t_group(phase, p, s)])
        for h, d in HD:
            if s == 1:
                go(T[h, phase, p, 2, d])

    def share(*rs):
        for r in rs:
            go(S[r])

    def split(src, hi, lo, hi8, lo8, first, last):
        def step(i, _):
            rows = pl.ds(pl.multiple_of(first + i * 32, 32), 32)
            v = src[rows, :] * UP
            top = v.astype(BF16)
            rest = v - top.astype(F32)
            hi[rows, :] = top
            lo[rows, :] = rest.astype(BF16)
            hi8[rows, :] = (v * 0.0625).astype(F8)
            lo8[rows, :] = (rest * 16.0).astype(F8)
            return 0

        lax.fori_loop(0, (last - first) // 32, step, 0)

    def split_i(first, last):
        split(img, ih, il, ih8, il8, first, last)

    def split_t(first, last):
        split(txt, th, tl, th8, tl8, first, last)

    def block(i0, i1, t0, t1, first_i=False, first_t=False, across=False, flip=False, hooks=()):
        hooks = dict(enumerate(hooks))
        image = (ih, il, ih8, il8, d_img, rid_i, cid_i, slice(i0, i1), first_i)
        text = (th, tl, th8, tl8, d_txt, rid_t, cid_t, slice(t0, t1), first_t)
        (a_hi, a_lo, a_hi8, a_lo8, d_a, rid, _, ra, first_a) = text if across else image
        (b_hi, b_lo, b_hi8, b_lo8, d_b, _, cid, rb, first_b) = image if across else text
        na, nb = ra.stop - ra.start, rb.stop - rb.start
        s_ref[ra, rb] = dot(jnp.concatenate([a_hi[ra, :], a_lo[ra, :], a_hi[ra, :]], 1),
                            jnp.concatenate([b_hi[rb, :], b_hi[rb, :], b_lo[rb, :]], 1), NT)
        if 0 in hooks:
            hooks[0]()
        n = max(16384 // nb // 32, 1) * 32
        sums = [jnp.zeros((8, nb), F32)] * 3
        for b in range(ra.start, ra.stop, n):
            rows = slice(b, b + n)
            scores = s_ref[rows, rb]
            row = jnp.concatenate([rid[rows, :]] * (nb // 128), 1)
            same = row == jnp.concatenate([cid[:, rb]] * (n // 8), 0)
            losses, slopes = pair_terms(scores, same, warm_down, offset)
            sums = [u + jnp.sum(v.reshape(n // 8, 8, nb), axis=0) for u, v in zip(sums, (losses, slopes * scores, slopes))]
            slopes = slopes * UP
            hi = slopes.astype(BF16)
            sh_ref[rows, rb] = hi
            sh8_ref[rows, rb] = (slopes * 0.0625).astype(F8)
            sl8_ref[rows, rb] = ((slopes - hi.astype(F32)) * 16.0).astype(F8)
        for k, v in enumerate(sums):
            acc[k] += sum(v[:, q:q + 128] for q in range(0, nb, 128))
        if 1 in hooks:
            hooks[1]()
        sh, sh8, sl8 = sh_ref[ra, rb], sh8_ref[ra, rb], sl8_ref[ra, rb]

        def down():
            g = dot(sh, b_hi[rb, :], NN) + dot(jnp.concatenate([sl8, sh8], 1), jnp.concatenate([b_hi8[rb, :], b_lo8[rb, :]], 0), NN)
            d_a[ra, :] = g if first_a else d_a[ra, :] + g

        def over():
            g = dot(sh, a_hi[ra, :], TN) + dot(jnp.concatenate([sl8, sh8], 0), jnp.concatenate([a_hi8[ra, :], a_lo8[ra, :]], 0), TN)
            d_b[rb, :] = g if first_b else d_b[rb, :] + g

        (over if flip else down)()
        if 2 in hooks:
            hooks[2]()
        (down if flip else over)()

    for n in (0, 1):
        for d in (0, 1):
            go(Z[1, d, n if d == 0 else 1 - n])
    for h, d in HD:
        go(T[h, 0, 0, 1, d])
    for h, d in HD:
        go(T[h, 1, 0, 1, d])
    share(0)

    lane = lax.broadcasted_iota(jnp.int32, (8, 128), 1)
    for r in range(NZ):
        number = (((z + NZ - r) % NZ) * NX + x) * (2 * NY) + y * 2
        base = image_row(0, r)
        for k in (0, 1):
            rows = lax.broadcasted_iota(jnp.int32, (SHARD, 128), 0)
            rid_i[base + k * SHARD:base + (k + 1) * SHARD, :] = (number + (c + k) % 2) * SHARD + rows
        own, other = (number + c) * SHARD + lane, (number + (c + 1) % 2) * SHARD + lane - SHARD
        cid_i[:, base:base + 128] = jnp.where(lane < SHARD, own, other)
    for part in range(ROWS // 128):
        ids = jnp.zeros((8, 128), jnp.int32)
        for h in (0, 1):
            for p in range(4):
                for q in range(4):
                    pos = text_row(h, p, q)
                    if pos // 128 == part:
                        a, b = (p, q) if h == 0 else (q, p)
                        number = (((y + NY - b) % NY) * 2 + c) * (NX * NZ) + z * NX + (x + NX - a) % NX
                        off = pos % 128
                        inside = (lane >= off) & (lane < off + HALF)
                        ids = jnp.where(inside, number * SHARD + h * HALF + lane - off, ids)
                        rows = lax.broadcasted_iota(jnp.int32, (HALF, 128), 0)
                        rid_t[pos:pos + HALF, :] = number * SHARD + h * HALF + rows
        cid_t[:, part * 128:(part + 1) * 128] = ids
    acc[...] = jnp.zeros_like(acc)

    pass_t(0, 0, 1)
    for p in (1, 3):
        for h in (0, 1):
            for d in (0, 1):
                go(T[h, 1, p, 1, d])
    pass_z(1, 0)
    landed(SHARD, sr.at[0])
    split_i(0, 128)
    pass_z(1, 1)
    share(1, 7)
    pass_t(0, 0, 2)
    for h in (0, 1):
        for d in (0, 1):
            go(T[h, 1, 2, 1, d])
    split_t(0, 256)
    pass_z(2, 0)
    landed(2 * SHARD, sr.at[1])
    split_i(128, 384)
    pass_t(1, 0, 1)
    pass_t(1, 1, 1)
    split_t(256, 512)

    def nothing():
        pass

    def take_2():
        pass_z(2, 1)
        share(2, 6)

    def take_4():
        landed(2 * HALF, zr.at[6])
        share(4)

    block(0, 384, 0, 512, True, True, hooks=(take_2, nothing, lambda: pass_t(1, 3, 1)))
    pass_z(3, 0)
    landed(2 * SHARD, sr.at[2])
    split_i(384, 640)
    block(384, 640, 0, 512, True, hooks=(nothing, lambda: pass_t(1, 2, 1)))
    pass_z(3, 1)
    share(3, 5)
    split_t(512, 768)
    block(0, 640, 512, 768, False, True, across=True, hooks=(nothing, nothing, take_4))
    for p in (0, 1, 3, 2):
        pass_t(1, p, 2)
    split_t(768, 1024)
    landed(3 * SHARD, sr.at[3])
    split_i(640, 1024)
    for k, rows in enumerate((14 * HALF, NZ * SHARD, 15 * SHARD)):
        landed(rows, sent.at[k])

    def rs_copy(r):
        return remote(d_img.at[pl.ds(image_row(1, r), SHARD)], got_s.at[r], sent.at[1], rsr.at[BACK[r]], near["s"])

    def rz_copy(s, d, h):
        r = s if d == 0 else 8 - s
        return remote(d_img.at[pl.ds(image_row(0, r) + h * HALF, HALF)], got_z.at[s - 1, d, pl.ds(h * HALF, HALF)],
                      sent.at[0], rzr.at[z_group(s, 1 - d, h)], near["z-" if d == 0 else "z+"])

    def rt_copy(h, phase, p, s, d):
        q = s if d == 0 else 4 - s
        off, n = (0, HALF) if s < 2 else ((0, QUARTER) if d == 0 else (QUARTER, QUARTER))
        a = text_row(h, q, 0) if phase == 0 else text_row(h, p, q)
        i = t_index(h, phase, p, s, d)
        axis = ("xy", "yx")[h][phase]
        return remote(d_txt.at[pl.ds(a + off, n)], got_t.at[i, pl.ds(0, n)], sent.at[2], rtr.at[t_group(phase, p, s)], near[axis + ("-" if d == 0 else "+")])

    RT = {k: rt_copy(*k) for k in keys}
    RZ = {k: rz_copy(*k) for k in z_keys}
    RS = {r: rs_copy(r) for r in range(NZ)}

    def add_t(h, phase, p, s, d):
        q = s - 1 if d == 0 else (5 - s) % 4
        off, n = (0, HALF) if s < 2 else ((0, QUARTER) if d == 0 else (QUARTER, QUARTER))
        a = (text_row(h, q, 0) if phase == 0 else text_row(h, p, q)) + off
        d_txt[a:a + n, :] += got_t[t_index(h, phase, p, s, d), 0:n, :]

    def add_z(s, d, h):
        r = s - 1 if d == 0 else (9 - s) % 8
        a = image_row(0, r) + h * HALF
        d_img[a:a + HALF, :] += got_z[s - 1, d, h * HALF:(h + 1) * HALF, :]

    def add_s(r):
        a = image_row(0, r)
        d_img[a:a + SHARD, :] += got_s[r]

    def back_t(phase, p, s, then=None):
        landed(4 * HALF if s == 1 else 4 * QUARTER, rtr.at[t_group(phase, p, s)])
        for h, d in HD:
            add_t(h, phase, p, s, d)
            if then is not None:
                go(RT[(h,) + then + (d,)])

    def back_z(s, n):
        landed(2 * HALF, rzr.at[z_group(s, 0, n)])
        for d in (0, 1):
            h = (1 - n if d == 0 else n) if s < 4 else d
            add_z(s, d, h)
            if s > 1:
                go(RZ[s - 1, d, h])

    STAGES = ((0, NZ, lambda k: at(dz=k)), (7, NX, lambda k: at(dx=k)), (10, NY, lambda k: at(dy=k)), (13, 2, lambda k: at(dc=k)))

    def fan(stage):
        base, size, where = STAGES[stage]
        for k in range(1, size):
            go(remote(sum_own.at[stage], sum_got.at[base + k - 1], sent.at[3], qr.at[stage], where(k)))

    def fold(stage):
        base, size, _ = STAGES[stage]
        got = sum_got.at[pl.ds(base, size - 1)]
        pltpu.make_async_copy(got, got, qr.at[stage]).wait()
        total = sum_own[stage]
        for k in range(base, base + size - 1):
            total = total + sum_got[k]
        sum_own[stage + 1] = total

    d_img[640:1024, :] = jnp.zeros((384, D), F32)

    def send_far():
        for p in (2, 1, 3, 0):
            for h, d in HD:
                go(RT[h, 1, p, 2, d])

    block(0, 1024, 768, 1024, False, True, across=True, hooks=(nothing, nothing, send_far))
    block(896, 1024, 0, 768, hooks=(nothing, nothing, lambda: go(RS[4])))

    def start_z():
        landed(SHARD, rsr.at[0])
        add_s(4)
        for d in (0, 1):
            go(RZ[4, d, d])

    def near_t():
        for p in (2, 1, 3, 0):
            back_t(1, p, 2, (1, p, 1))

    block(640, 896, 0, 768, flip=True, hooks=(start_z, nothing, near_t))
    for r in (3, 5, 2, 6, 1, 7, 0):
        go(RS[r])
    for k in range(3):
        sum_own[0, k:k + 1, :] = jnp.sum(acc[k], axis=0, keepdims=True)
    sum_own[0, 3:8, :] = jnp.zeros((5, 128), F32)
    fan(0)
    landed(2 * SHARD, rsr.at[1])
    for r in (3, 5):
        add_s(r)
    for d in (0, 1):
        go(RZ[3, d, 1 - d])
    back_z(4, 0)
    landed(5 * SHARD, rsr.at[2])
    for r in (2, 6, 1, 7, 0):
        add_s(r)
    fold(0)
    fan(1)
    back_z(3, 0)
    back_t(1, 2, 1)
    for h, d in HD:
        go(RT[h, 0, 0, 2, d])
    back_z(3, 1)
    fold(1)
    fan(2)
    back_t(1, 1, 1)
    back_z(2, 0)
    back_t(1, 3, 1)
    back_t(0, 0, 2, (0, 0, 1))
    back_z(2, 1)
    fold(2)
    fan(3)
    back_z(1, 0)
    back_t(1, 0, 1)
    back_z(1, 1)
    o_pic[...] = project_back(pic_unit, pic_norm, warm_down * d_img[own_i:own_i + SHARD, :])
    fold(3)
    totals = jnp.sum(sum_own[4], axis=1, keepdims=True) * (1.0 / 16384.0)
    kind = lax.broadcasted_iota(jnp.int32, (8, 1), 0)
    o_sum[...] = jnp.broadcast_to(jnp.where(kind == 1, warm_down * totals, totals), (8, 128))
    back_t(0, 0, 1)
    grads = jnp.concatenate([d_txt[text_row(h, 0, 0):text_row(h, 0, 0) + HALF, :] for h in (0, 1)], 0)
    o_cap[...] = project_back(cap_unit, cap_norm, warm_down * grads)
    for k, rows in enumerate((14 * HALF, NZ * SHARD, 15 * SHARD)):
        landed(rows, sent.at[k])
    pltpu.make_async_copy(sum_got, sum_got, sent.at[3]).wait()


def finish(sums, pic, cap, o_loss, o_pic, o_cap, o_warmth, o_bias):
    o_loss[...] = sums[0:1, 0:1]
    o_warmth[...] = sums[1:2, 0:1]
    o_bias[...] = sums[2:3, 0:1]
    o_pic[...] = pic[...]
    o_cap[...] = cap[...]


def body(picture_vectors, caption_vectors, warmth_exponent, offset_weight):
    vmem, smem = pl.BlockSpec(memory_space=pltpu.VMEM), pl.BlockSpec(memory_space=pltpu.SMEM)
    dma = pltpu.SemaphoreType.DMA
    big, split, eighth = pltpu.VMEM((ROWS, D), F32), pltpu.VMEM((ROWS, D), BF16), pltpu.VMEM((ROWS, D), F8)
    one, shard = jax.ShapeDtypeStruct((1, 1), F32), jax.ShapeDtypeStruct((SHARD, D), F32)
    results = pl.pallas_call(
        kernel,
        out_shape=[jax.ShapeDtypeStruct((8, 128), F32), shard, shard],
        in_specs=[vmem, vmem, smem, smem],
        out_specs=[vmem] * 3,
        scratch_shapes=[
            big, big, split, split, split, split, eighth, eighth, eighth, eighth, big, big,
            pltpu.VMEM((ROWS, ROWS), F32), pltpu.VMEM((ROWS, ROWS), BF16), pltpu.VMEM((ROWS, ROWS), F8), pltpu.VMEM((ROWS, ROWS), F8),
            pltpu.VMEM((ROWS, 128), jnp.int32), pltpu.VMEM((8, ROWS), jnp.int32), pltpu.VMEM((ROWS, 128), jnp.int32),
            pltpu.VMEM((8, ROWS), jnp.int32), pltpu.VMEM((3, 8, 128), F32),
            pltpu.VMEM((NZ, SHARD, D), F32), pltpu.VMEM((4, 2, SHARD, D), F32), pltpu.VMEM((40, HALF, D), F32),
            pltpu.VMEM((5, 8, 128), F32), pltpu.VMEM((14, 8, 128), F32),
            dma((7,)), dma((4,)), dma((10,)), dma((7,)), dma((3,)), dma((10,)), dma((4,)), dma((4,)),
        ],
        compiler_params=pltpu.CompilerParams(collective_id=0, has_side_effects=True, vmem_limit_bytes=62 * 2**20),
    )(picture_vectors, caption_vectors, warmth_exponent, offset_weight)
    loss, picture_derivative, caption_derivative, warmth, bias = pl.pallas_call(
        finish, out_shape=[one, shard, shard, one, one], in_specs=[vmem] * 3, out_specs=[vmem] * 5
    )(*results)
    return loss.reshape(1), picture_derivative, caption_derivative, warmth.reshape(1), bias.reshape(1)


def solution(mesh):
    in_specs = (P(("img", "txt"), None), P(("txt", "img"), None), P(), P())
    out_specs = (P(), P(("img", "txt"), None), P(("txt", "img"), None), P(), P())
    return jax.shard_map(body, mesh=mesh, in_specs=in_specs, out_specs=out_specs, check_vma=False)
```

```python
import functools

import jax
import jax.numpy as jnp
from jax import lax
from jax.experimental import pallas as pl
from jax.experimental.pallas import tpu as pltpu
from jax.sharding import PartitionSpec as P

MESH = pl.DeviceIdType.MESH
F32, BF16, F8 = jnp.float32, jnp.bfloat16, jnp.float8_e4m3fn
UP = 4096.0
NX, NY, NZ = 4, 4, 8
SHARD, HALF, QUARTER, D = 64, 32, 16, 1152
ROWS = 1024
SHARE = {0: 0, 1: 1, 7: 1, 2: 2, 6: 2, 3: 3, 5: 3, 4: 4}
BACK = {4: 0, 5: 0, 3: 1, 6: 1, 2: 2, 1: 2, 7: 2, 0: 2}
NT = (((1,), (1,)), ((), ()))
NN = (((1,), (0,)), ((), ()))
TN = (((0,), (0,)), ((), ()))


def dot(a, b, dims):
    return lax.dot_general(a, b, dims, preferred_element_type=F32)


def image_row(k, r):
    return {0: 0, 1: 128, 7: 256, 2: 384, 6: 512, 3: 640, 5: 768, 4: 896}[r] + k * SHARD


def text_row(h, p, q):
    if q == 0:
        at = h * 4 + p
    elif q == 2:
        at = 24 + h * 4 + p
    else:
        at = 8 + (0, 1, 3, 2)[p] * 4 + h * 2 + (q == 3)
    return at * HALF


def unit_rows(values):
    norm = jnp.sqrt(jnp.sum(values * values, axis=1, keepdims=True) + 1e-06)
    return values / norm, norm


def project_back(unit, norm, grads):
    inner = jnp.sum(unit * grads, axis=1, keepdims=True)
    return (grads - unit * inner) / norm


def pair_terms(scores, same, temperature, offset):
    logits = temperature * scores + offset
    e = jnp.exp(logits)
    u = 1.0 + e
    r = 1.0 / u
    slopes = jnp.where(same, -r, e * r)
    g = jnp.where(same, 1.0 / e, e)
    small = g * (1.0 - g * (0.5 - g * (1.0 / 3.0)))
    losses = jnp.where(g < 0.015625, small, jnp.log(1.0 + g))
    return losses, slopes


def kernel(pic, cap, warmth, bias, o_sum, o_pic, o_cap,
           img, txt, ih, il, th, tl, ih8, il8, th8, tl8, d_img, d_txt, s_ref, sh_ref, sh8_ref, sl8_ref, rid_i, cid_i, rid_t, cid_t, acc,
           got_s, got_z, got_t, sum_own, sum_got, pic_own, cap_own, load, zr, sr, tr, rzr, rsr, rtr, qr, sent):
    loads = [pltpu.make_async_copy(src, dst, load.at[k]) for k, (src, dst) in enumerate(((pic, pic_own), (cap, cap_own)))]
    for copy in loads:
        copy.start()
    im = lax.axis_index("img")
    tx = lax.axis_index("txt")
    z, x = im // NX, im % NX
    y, c = tx // 2, tx % 2

    def at(dx=0, dy=0, dz=0, dc=0):
        return (((z + dz) % NZ) * NX + (x + dx) % NX, ((y + dy) % NY) * 2 + (c + dc) % 2)

    near = {"x+": at(dx=1), "x-": at(dx=3), "y+": at(dy=1), "y-": at(dy=3), "z+": at(dz=1), "z-": at(dz=7), "s": at(dc=1)}
    others = list(near.values()) + [at(dz=k) for k in (2, 3, 4, 5, 6)] + [at(dx=2), at(dy=2)]
    barrier = pltpu.get_barrier_semaphore()
    for other in others:
        pl.semaphore_signal(barrier, inc=1, device_id=other, device_id_type=MESH)

    for copy in loads:
        copy.wait()
    pic_unit, pic_norm = unit_rows(pic_own[...])
    cap_unit, cap_norm = unit_rows(cap_own[...])
    own_i = image_row(0, 0)
    img[own_i:own_i + SHARD, :] = pic_unit
    for h in (0, 1):
        t0 = text_row(h, 0, 0)
        txt[t0:t0 + HALF, :] = cap_unit[h * HALF:(h + 1) * HALF, :]
    temperature = jnp.exp(jnp.full((1, 1), warmth[0], F32))
    offset = jnp.full((1, 1), bias[0], F32)
    warm_down = temperature * (1.0 / (UP * UP))

    pl.semaphore_wait(barrier, len(others))

    def remote(src, dst, s, r, dev):
        return pltpu.make_async_remote_copy(src_ref=src, dst_ref=dst, send_sem=s, recv_sem=r, device_id=dev, device_id_type=MESH)

    def landed(rows, sem):
        pltpu.make_async_copy(d_img.at[pl.ds(0, rows)], d_img.at[pl.ds(0, rows)], sem).wait()

    def go(copy):
        copy.start()

    def z_group(s, d, h):
        return (s - 1) * 2 + ((h if d == 0 else 1 - h) if s < 4 else 0)

    def t_group(phase, p, s):
        return (0 if phase == 0 else 2 + 2 * p) + s - 1

    def z_copy(s, d, h):
        src, dst = ((s - 1), s) if d == 0 else ((9 - s) % 8, 8 - s)
        return remote(img.at[pl.ds(image_row(0, src) + h * HALF, HALF)], img.at[pl.ds(image_row(0, dst) + h * HALF, HALF)],
                      sent.at[0], zr.at[z_group(s, d, h)], near["z+" if d == 0 else "z-"])

    def s_copy(r):
        return remote(img.at[pl.ds(image_row(0, r), SHARD)], img.at[pl.ds(image_row(1, r), SHARD)], sent.at[1], sr.at[SHARE[r]], near["s"])

    def t_index(h, phase, p, s, d):
        return h * 20 + (0 if phase == 0 else 4 + p * 4) + (s - 1) * 2 + d

    def t_copy(h, phase, p, s, d):
        src, dst = (s - 1, s) if d == 0 else ((5 - s) % 4, 4 - s)
        off, n = (0, HALF) if s < 2 else ((0, QUARTER) if d == 0 else (QUARTER, QUARTER))
        a, b = (text_row(h, src, 0), text_row(h, dst, 0)) if phase == 0 else (text_row(h, p, src), text_row(h, p, dst))
        axis = ("xy", "yx")[h][phase]
        return remote(txt.at[pl.ds(a + off, n)], txt.at[pl.ds(b + off, n)], sent.at[2], tr.at[t_group(phase, p, s)], near[axis + ("+" if d == 0 else "-")])

    keys = [(h, 0, 0, s, d) for h in (0, 1) for s in (1, 2) for d in (0, 1)]
    keys += [(h, 1, p, s, d) for h in (0, 1) for p in range(4) for s in (1, 2) for d in (0, 1)]
    z_keys = [(s, d, h) for s in (1, 2, 3) for d in (0, 1) for h in (0, 1)] + [(4, 0, 0), (4, 1, 1)]
    T = {k: t_copy(*k) for k in keys}
    Z = {k: z_copy(*k) for k in z_keys}
    S = {r: s_copy(r) for r in range(NZ)}
    HD = [(h, d) for d in (0, 1) for h in (0, 1)]

    def pass_z(s, n):
        landed(2 * HALF, zr.at[z_group(s, 0, n)])
        for d in (0, 1):
            h = n if d == 0 else 1 - n
            if (s + 1, d, h) in Z:
                go(Z[s + 1, d, h])

    def pass_t(phase, p, s):
        landed(4 * HALF if s == 1 else 4 * QUARTER, tr.at[t_group(phase, p, s)])
        for h, d in HD:
            if s == 1:
                go(T[h, phase, p, 2, d])

    def share(*rs):
        for r in rs:
            go(S[r])

    def split(src, hi, lo, hi8, lo8, first, last):
        def step(i, _):
            rows = pl.ds(pl.multiple_of(first + i * 32, 32), 32)
            v = src[rows, :] * UP
            top = v.astype(BF16)
            rest = v - top.astype(F32)
            hi[rows, :] = top
            lo[rows, :] = rest.astype(BF16)
            hi8[rows, :] = (v * 0.0625).astype(F8)
            lo8[rows, :] = (rest * 16.0).astype(F8)
            return 0

        lax.fori_loop(0, (last - first) // 32, step, 0)

    def split_i(first, last):
        split(img, ih, il, ih8, il8, first, last)

    def split_t(first, last):
        split(txt, th, tl, th8, tl8, first, last)

    def block(i0, i1, t0, t1, first_i=False, first_t=False, across=False, flip=False, hooks=()):
        hooks = dict(enumerate(hooks))
        image = (ih, il, ih8, il8, d_img, rid_i, cid_i, slice(i0, i1), first_i)
        text = (th, tl, th8, tl8, d_txt, rid_t, cid_t, slice(t0, t1), first_t)
        (a_hi, a_lo, a_hi8, a_lo8, d_a, rid, _, ra, first_a) = text if across else image
        (b_hi, b_lo, b_hi8, b_lo8, d_b, _, cid, rb, first_b) = image if across else text
        na, nb = ra.stop - ra.start, rb.stop - rb.start
        s_ref[ra, rb] = dot(jnp.concatenate([a_hi[ra, :], a_lo[ra, :], a_hi[ra, :]], 1),
                            jnp.concatenate([b_hi[rb, :], b_hi[rb, :], b_lo[rb, :]], 1), NT)
        if 0 in hooks:
            hooks[0]()
        n = max(16384 // nb // 32, 1) * 32
        sums = [jnp.zeros((8, nb), F32)] * 3
        for b in range(ra.start, ra.stop, n):
            rows = slice(b, b + n)
            scores = s_ref[rows, rb]
            row = jnp.concatenate([rid[rows, :]] * (nb // 128), 1)
            same = row == jnp.concatenate([cid[:, rb]] * (n // 8), 0)
            losses, slopes = pair_terms(scores, same, warm_down, offset)
            sums = [u + jnp.sum(v.reshape(n // 8, 8, nb), axis=0) for u, v in zip(sums, (losses, slopes * scores, slopes))]
            slopes = slopes * UP
            hi = slopes.astype(BF16)
            sh_ref[rows, rb] = hi
            sh8_ref[rows, rb] = (slopes * 0.0625).astype(F8)
            sl8_ref[rows, rb] = ((slopes - hi.astype(F32)) * 16.0).astype(F8)
        for k, v in enumerate(sums):
            acc[k] += sum(v[:, q:q + 128] for q in range(0, nb, 128))
        if 1 in hooks:
            hooks[1]()
        sh, sh8, sl8 = sh_ref[ra, rb], sh8_ref[ra, rb], sl8_ref[ra, rb]

        def down():
            g = dot(sh, b_hi[rb, :], NN) + dot(jnp.concatenate([sl8, sh8], 1), jnp.concatenate([b_hi8[rb, :], b_lo8[rb, :]], 0), NN)
            d_a[ra, :] = g if first_a else d_a[ra, :] + g

        def over():
            g = dot(sh, a_hi[ra, :], TN) + dot(jnp.concatenate([sl8, sh8], 0), jnp.concatenate([a_hi8[ra, :], a_lo8[ra, :]], 0), TN)
            d_b[rb, :] = g if first_b else d_b[rb, :] + g

        (over if flip else down)()
        if 2 in hooks:
            hooks[2]()
        (down if flip else over)()

    for n in (0, 1):
        for d in (0, 1):
            go(Z[1, d, n if d == 0 else 1 - n])
    for h, d in HD:
        go(T[h, 0, 0, 1, d])
    for h, d in HD:
        go(T[h, 1, 0, 1, d])
    share(0)

    lane = lax.broadcasted_iota(jnp.int32, (8, 128), 1)
    for r in range(NZ):
        number = (((z + NZ - r) % NZ) * NX + x) * (2 * NY) + y * 2
        base = image_row(0, r)
        for k in (0, 1):
            rows = lax.broadcasted_iota(jnp.int32, (SHARD, 128), 0)
            rid_i[base + k * SHARD:base + (k + 1) * SHARD, :] = (number + (c + k) % 2) * SHARD + rows
        own, other = (number + c) * SHARD + lane, (number + (c + 1) % 2) * SHARD + lane - SHARD
        cid_i[:, base:base + 128] = jnp.where(lane < SHARD, own, other)
    for part in range(ROWS // 128):
        ids = jnp.zeros((8, 128), jnp.int32)
        for h in (0, 1):
            for p in range(4):
                for q in range(4):
                    pos = text_row(h, p, q)
                    if pos // 128 == part:
                        a, b = (p, q) if h == 0 else (q, p)
                        number = (((y + NY - b) % NY) * 2 + c) * (NX * NZ) + z * NX + (x + NX - a) % NX
                        off = pos % 128
                        inside = (lane >= off) & (lane < off + HALF)
                        ids = jnp.where(inside, number * SHARD + h * HALF + lane - off, ids)
                        rows = lax.broadcasted_iota(jnp.int32, (HALF, 128), 0)
                        rid_t[pos:pos + HALF, :] = number * SHARD + h * HALF + rows
        cid_t[:, part * 128:(part + 1) * 128] = ids
    acc[...] = jnp.zeros_like(acc)

    pass_t(0, 0, 1)
    for p in (1, 3):
        for h in (0, 1):
            for d in (0, 1):
                go(T[h, 1, p, 1, d])
    pass_z(1, 0)
    landed(SHARD, sr.at[0])
    split_i(0, 128)
    pass_z(1, 1)
    share(1, 7)
    pass_t(0, 0, 2)
    for h in (0, 1):
        for d in (0, 1):
            go(T[h, 1, 2, 1, d])
    split_t(0, 256)
    pass_z(2, 0)
    landed(2 * SHARD, sr.at[1])
    split_i(128, 384)
    pass_t(1, 0, 1)
    pass_t(1, 1, 1)
    split_t(256, 512)

    def nothing():
        pass

    def take(s, n, *rs):
        def hook():
            pass_z(s, n)
            share(*rs)

        return hook

    def take_4():
        landed(2 * HALF, zr.at[6])
        share(4)

    block(0, 256, 0, 512, True, True, hooks=(take(2, 1, 2, 6), nothing, lambda: pass_t(1, 3, 1)))
    landed(2 * SHARD, sr.at[2])
    split_i(384, 640)
    block(256, 512, 0, 512, True, hooks=(take(3, 0), nothing, lambda: pass_t(1, 2, 1)))
    split_t(512, 768)
    block(0, 512, 512, 768, False, True, across=True, hooks=(take(3, 1, 3, 5),))
    landed(2 * SHARD, sr.at[3])
    split_i(640, 896)
    block(512, 768, 0, 512, True, hooks=(nothing, take_4))
    for p in (0, 1, 3, 2):
        pass_t(1, p, 2)
    split_t(768, 1024)
    landed(SHARD, sr.at[4])
    split_i(896, 1024)
    for k, rows in enumerate((14 * HALF, NZ * SHARD, 15 * SHARD)):
        landed(rows, sent.at[k])

    def rs_copy(r):
        return remote(d_img.at[pl.ds(image_row(1, r), SHARD)], got_s.at[r], sent.at[1], rsr.at[BACK[r]], near["s"])

    def rz_copy(s, d, h):
        r = s if d == 0 else 8 - s
        return remote(d_img.at[pl.ds(image_row(0, r) + h * HALF, HALF)], got_z.at[s - 1, d, pl.ds(h * HALF, HALF)],
                      sent.at[0], rzr.at[z_group(s, 1 - d, h)], near["z-" if d == 0 else "z+"])

    def rt_copy(h, phase, p, s, d):
        q = s if d == 0 else 4 - s
        off, n = (0, HALF) if s < 2 else ((0, QUARTER) if d == 0 else (QUARTER, QUARTER))
        a = text_row(h, q, 0) if phase == 0 else text_row(h, p, q)
        i = t_index(h, phase, p, s, d)
        axis = ("xy", "yx")[h][phase]
        return remote(d_txt.at[pl.ds(a + off, n)], got_t.at[i, pl.ds(0, n)], sent.at[2], rtr.at[t_group(phase, p, s)], near[axis + ("-" if d == 0 else "+")])

    RT = {k: rt_copy(*k) for k in keys}
    RZ = {k: rz_copy(*k) for k in z_keys}
    RS = {r: rs_copy(r) for r in range(NZ)}

    def add_t(h, phase, p, s, d):
        q = s - 1 if d == 0 else (5 - s) % 4
        off, n = (0, HALF) if s < 2 else ((0, QUARTER) if d == 0 else (QUARTER, QUARTER))
        a = (text_row(h, q, 0) if phase == 0 else text_row(h, p, q)) + off
        d_txt[a:a + n, :] += got_t[t_index(h, phase, p, s, d), 0:n, :]

    def add_z(s, d, h):
        r = s - 1 if d == 0 else (9 - s) % 8
        a = image_row(0, r) + h * HALF
        d_img[a:a + HALF, :] += got_z[s - 1, d, h * HALF:(h + 1) * HALF, :]

    def add_s(r):
        a = image_row(0, r)
        d_img[a:a + SHARD, :] += got_s[r]

    def back_t(phase, p, s, then=None):
        landed(4 * HALF if s == 1 else 4 * QUARTER, rtr.at[t_group(phase, p, s)])
        for h, d in HD:
            add_t(h, phase, p, s, d)
            if then is not None:
                go(RT[(h,) + then + (d,)])

    def back_z(s, n):
        landed(2 * HALF, rzr.at[z_group(s, 0, n)])
        for d in (0, 1):
            h = (1 - n if d == 0 else n) if s < 4 else d
            add_z(s, d, h)
            if s > 1:
                go(RZ[s - 1, d, h])

    STAGES = ((0, NZ, lambda k: at(dz=k)), (7, NX, lambda k: at(dx=k)), (10, NY, lambda k: at(dy=k)), (13, 2, lambda k: at(dc=k)))

    def fan(stage):
        base, size, where = STAGES[stage]
        for k in range(1, size):
            go(remote(sum_own.at[stage], sum_got.at[base + k - 1], sent.at[3], qr.at[stage], where(k)))

    def fold(stage):
        base, size, _ = STAGES[stage]
        got = sum_got.at[pl.ds(base, size - 1)]
        pltpu.make_async_copy(got, got, qr.at[stage]).wait()
        total = sum_own[stage]
        for k in range(base, base + size - 1):
            total = total + sum_got[k]
        sum_own[stage + 1] = total

    d_img[768:1024, :] = jnp.zeros((256, D), F32)

    def send_far():
        for p in (2, 1, 3, 0):
            for h, d in HD:
                go(RT[h, 1, p, 2, d])

    block(0, 1024, 768, 1024, False, True, across=True, hooks=(nothing, nothing, send_far))
    for r in (2, 1, 7, 0):
        go(RS[r])

    def send_back():
        for r in (4, 5):
            go(RS[r])

    block(768, 1024, 0, 768, hooks=(nothing, nothing, send_back))

    def start_z():
        landed(2 * SHARD, rsr.at[0])
        add_s(4)
        add_s(5)
        for k in ((4, 0, 0), (4, 1, 1), (3, 1, 0)):
            go(RZ[k])

    def near_t():
        for p in (2, 1, 3, 0):
            back_t(1, p, 2, (1, p, 1))

    block(512, 768, 512, 768, flip=True, hooks=(start_z, nothing, near_t))
    for r in (3, 6):
        go(RS[r])
    for k in range(3):
        sum_own[0, k:k + 1, :] = jnp.sum(acc[k], axis=0, keepdims=True)
    sum_own[0, 3:8, :] = jnp.zeros((5, 128), F32)
    fan(0)
    landed(4 * SHARD, rsr.at[2])
    for r in (2, 1, 7, 0):
        add_s(r)
    landed(2 * SHARD, rsr.at[1])
    for r in (3, 6):
        add_s(r)
    go(RZ[3, 0, 1])
    back_z(4, 0)
    fold(0)
    fan(1)
    back_z(3, 0)
    back_t(1, 2, 1)
    for h, d in HD:
        go(RT[h, 0, 0, 2, d])
    back_z(3, 1)
    fold(1)
    fan(2)
    back_t(1, 1, 1)
    back_z(2, 0)
    back_t(1, 3, 1)
    back_t(0, 0, 2, (0, 0, 1))
    back_z(2, 1)
    fold(2)
    fan(3)
    back_z(1, 0)
    back_t(1, 0, 1)
    back_z(1, 1)
    o_pic[...] = project_back(pic_unit, pic_norm, warm_down * d_img[own_i:own_i + SHARD, :])
    fold(3)
    totals = jnp.sum(sum_own[4], axis=1, keepdims=True) * (1.0 / 16384.0)
    kind = lax.broadcasted_iota(jnp.int32, (8, 1), 0)
    o_sum[...] = jnp.broadcast_to(jnp.where(kind == 1, warm_down * totals, totals), (8, 128))
    back_t(0, 0, 1)
    grads = jnp.concatenate([d_txt[text_row(h, 0, 0):text_row(h, 0, 0) + HALF, :] for h in (0, 1)], 0)
    o_cap[...] = project_back(cap_unit, cap_norm, warm_down * grads)
    for k, rows in enumerate((14 * HALF, NZ * SHARD, 15 * SHARD)):
        landed(rows, sent.at[k])
    pltpu.make_async_copy(sum_got, sum_got, sent.at[3]).wait()


def finish(sums, pic, cap, o_loss, o_pic, o_cap, o_warmth, o_bias):
    o_loss[...] = sums[0:1, 0:1]
    o_warmth[...] = sums[1:2, 0:1]
    o_bias[...] = sums[2:3, 0:1]
    o_pic[...] = pic[...]
    o_cap[...] = cap[...]


def body(picture_vectors, caption_vectors, warmth_exponent, offset_weight):
    vmem, smem, hbm = (pl.BlockSpec(memory_space=m) for m in (pltpu.VMEM, pltpu.SMEM, pl.ANY))
    dma = pltpu.SemaphoreType.DMA
    big, split, eighth = pltpu.VMEM((ROWS, D), F32), pltpu.VMEM((ROWS, D), BF16), pltpu.VMEM((ROWS, D), F8)
    one, shard = jax.ShapeDtypeStruct((1, 1), F32), jax.ShapeDtypeStruct((SHARD, D), F32)
    results = pl.pallas_call(
        kernel,
        out_shape=[jax.ShapeDtypeStruct((8, 128), F32), shard, shard],
        in_specs=[hbm, hbm, smem, smem],
        out_specs=[vmem] * 3,
        scratch_shapes=[
            big, big, split, split, split, split, eighth, eighth, eighth, eighth, big, big,
            pltpu.VMEM((ROWS, ROWS), F32), pltpu.VMEM((ROWS, ROWS), BF16), pltpu.VMEM((ROWS, ROWS), F8), pltpu.VMEM((ROWS, ROWS), F8),
            pltpu.VMEM((ROWS, 128), jnp.int32), pltpu.VMEM((8, ROWS), jnp.int32), pltpu.VMEM((ROWS, 128), jnp.int32),
            pltpu.VMEM((8, ROWS), jnp.int32), pltpu.VMEM((3, 8, 128), F32),
            pltpu.VMEM((NZ, SHARD, D), F32), pltpu.VMEM((4, 2, SHARD, D), F32), pltpu.VMEM((40, HALF, D), F32),
            pltpu.VMEM((5, 8, 128), F32), pltpu.VMEM((14, 8, 128), F32), pltpu.VMEM((SHARD, D), F32), pltpu.VMEM((SHARD, D), F32), dma((2,)),
            dma((7,)), dma((5,)), dma((10,)), dma((7,)), dma((3,)), dma((10,)), dma((4,)), dma((4,)),
        ],
        compiler_params=pltpu.CompilerParams(collective_id=0, has_side_effects=True, vmem_limit_bytes=62 * 2**20),
    )(picture_vectors, caption_vectors, warmth_exponent, offset_weight)
    loss, picture_derivative, caption_derivative, warmth, bias = pl.pallas_call(
        finish, out_shape=[one, shard, shard, one, one], in_specs=[vmem] * 3, out_specs=[vmem] * 5
    )(*results)
    return loss.reshape(1), picture_derivative, caption_derivative, warmth.reshape(1), bias.reshape(1)


def solution(mesh):
    in_specs = (P(("img", "txt"), None), P(("txt", "img"), None), P(), P())
    out_specs = (P(), P(("img", "txt"), None), P(("txt", "img"), None), P(), P())
    return jax.shard_map(body, mesh=mesh, in_specs=in_specs, out_specs=out_specs, check_vma=False)
```

```python
import functools

import jax
import jax.numpy as jnp
from jax import lax
from jax.experimental import pallas as pl
from jax.experimental.pallas import tpu as pltpu
from jax.sharding import PartitionSpec as P

MESH = pl.DeviceIdType.MESH
F32, BF16, F8 = jnp.float32, jnp.bfloat16, jnp.float8_e4m3fn
UP = 4096.0
NX, NY, NZ = 4, 4, 8
SHARD, HALF, QUARTER, D = 64, 32, 16, 1152
ROWS = 1024
SHARE = {0: 0, 1: 1, 7: 1, 2: 2, 6: 2, 3: 3, 5: 3, 4: 4}
BACK = {4: 0, 5: 0, 3: 1, 6: 1, 2: 2, 1: 2, 7: 2, 0: 2}
NT = (((1,), (1,)), ((), ()))
NN = (((1,), (0,)), ((), ()))
TN = (((0,), (0,)), ((), ()))


def dot(a, b, dims):
    return lax.dot_general(a, b, dims, preferred_element_type=F32)


def image_row(k, r):
    return {0: 0, 1: 128, 7: 256, 2: 384, 6: 512, 3: 640, 5: 768, 4: 896}[r] + k * SHARD


def text_row(h, p, q):
    if q == 0:
        at = h * 4 + p
    elif q == 2:
        at = 24 + h * 4 + p
    else:
        at = 8 + (0, 1, 3, 2)[p] * 4 + h * 2 + (q == 3)
    return at * HALF


def unit_rows(values):
    norm = jnp.sqrt(jnp.sum(values * values, axis=1, keepdims=True) + 1e-06)
    return values / norm, norm


def project_back(unit, norm, grads):
    inner = jnp.sum(unit * grads, axis=1, keepdims=True)
    return (grads - unit * inner) / norm


def pair_terms(scores, same, temperature, offset):
    logits = temperature * scores + offset
    e = jnp.exp(logits)
    u = 1.0 + e
    r = 1.0 / u
    slopes = jnp.where(same, -r, e * r)
    g = jnp.where(same, 1.0 / e, e)
    small = g * (1.0 - g * (0.5 - g * (1.0 / 3.0)))
    losses = jnp.where(g < 0.015625, small, jnp.log(1.0 + g))
    return losses, slopes


def kernel(pic, cap, warmth, bias, o_sum, o_pic, o_cap,
           img, txt, ih, il, th, tl, ih8, il8, th8, tl8, d_img, d_txt, s_ref, sh_ref, sh8_ref, sl8_ref, rid_i, cid_i, rid_t, cid_t, acc,
           got_s, got_z, got_t, sum_own, sum_got, pic_own, cap_own, load, zr, sr, tr, rzr, rsr, rtr, qr, sent):
    loads = [pltpu.make_async_copy(src, dst, load.at[k]) for k, (src, dst) in enumerate(((pic, pic_own), (cap, cap_own)))]
    for copy in loads:
        copy.start()
    im = lax.axis_index("img")
    tx = lax.axis_index("txt")
    z, x = im // NX, im % NX
    y, c = tx // 2, tx % 2

    def at(dx=0, dy=0, dz=0, dc=0):
        return (((z + dz) % NZ) * NX + (x + dx) % NX, ((y + dy) % NY) * 2 + (c + dc) % 2)

    near = {"x+": at(dx=1), "x-": at(dx=3), "y+": at(dy=1), "y-": at(dy=3), "z+": at(dz=1), "z-": at(dz=7), "s": at(dc=1)}
    others = list(near.values()) + [at(dz=k) for k in (2, 3, 4, 5, 6)] + [at(dx=2), at(dy=2)]
    barrier = pltpu.get_barrier_semaphore()
    for other in others:
        pl.semaphore_signal(barrier, inc=1, device_id=other, device_id_type=MESH)

    for copy in loads:
        copy.wait()
    pic_unit, pic_norm = unit_rows(pic_own[...])
    cap_unit, cap_norm = unit_rows(cap_own[...])
    own_i = image_row(0, 0)
    img[own_i:own_i + SHARD, :] = pic_unit
    for h in (0, 1):
        t0 = text_row(h, 0, 0)
        txt[t0:t0 + HALF, :] = cap_unit[h * HALF:(h + 1) * HALF, :]
    temperature = jnp.exp(jnp.full((1, 1), warmth[0], F32))
    offset = jnp.full((1, 1), bias[0], F32)
    warm_down = temperature * (1.0 / (UP * UP))

    pl.semaphore_wait(barrier, len(others))

    def remote(src, dst, s, r, dev):
        return pltpu.make_async_remote_copy(src_ref=src, dst_ref=dst, send_sem=s, recv_sem=r, device_id=dev, device_id_type=MESH)

    def landed(rows, sem):
        pltpu.make_async_copy(d_img.at[pl.ds(0, rows)], d_img.at[pl.ds(0, rows)], sem).wait()

    def go(copy):
        copy.start()

    def z_group(s, d, h):
        return (s - 1) * 2 + ((h if d == 0 else 1 - h) if s < 4 else 0)

    def t_group(phase, p, s):
        return (0 if phase == 0 else 2 + 2 * p) + s - 1

    def z_copy(s, d, h):
        src, dst = ((s - 1), s) if d == 0 else ((9 - s) % 8, 8 - s)
        return remote(img.at[pl.ds(image_row(0, src) + h * HALF, HALF)], img.at[pl.ds(image_row(0, dst) + h * HALF, HALF)],
                      sent.at[0], zr.at[z_group(s, d, h)], near["z+" if d == 0 else "z-"])

    def s_copy(r):
        return remote(img.at[pl.ds(image_row(0, r), SHARD)], img.at[pl.ds(image_row(1, r), SHARD)], sent.at[1], sr.at[SHARE[r]], near["s"])

    def t_index(h, phase, p, s, d):
        return h * 20 + (0 if phase == 0 else 4 + p * 4) + (s - 1) * 2 + d

    def t_copy(h, phase, p, s, d):
        src, dst = (s - 1, s) if d == 0 else ((5 - s) % 4, 4 - s)
        off, n = (0, HALF) if s < 2 else ((0, QUARTER) if d == 0 else (QUARTER, QUARTER))
        a, b = (text_row(h, src, 0), text_row(h, dst, 0)) if phase == 0 else (text_row(h, p, src), text_row(h, p, dst))
        axis = ("xy", "yx")[h][phase]
        return remote(txt.at[pl.ds(a + off, n)], txt.at[pl.ds(b + off, n)], sent.at[2], tr.at[t_group(phase, p, s)], near[axis + ("+" if d == 0 else "-")])

    keys = [(h, 0, 0, s, d) for h in (0, 1) for s in (1, 2) for d in (0, 1)]
    keys += [(h, 1, p, s, d) for h in (0, 1) for p in range(4) for s in (1, 2) for d in (0, 1)]
    z_keys = [(s, d, h) for s in (1, 2, 3) for d in (0, 1) for h in (0, 1)] + [(4, 0, 0), (4, 1, 1)]
    T = {k: t_copy(*k) for k in keys}
    Z = {k: z_copy(*k) for k in z_keys}
    S = {r: s_copy(r) for r in range(NZ)}
    HD = [(h, d) for d in (0, 1) for h in (0, 1)]

    def pass_z(s, n):
        landed(2 * HALF, zr.at[z_group(s, 0, n)])
        for d in (0, 1):
            h = n if d == 0 else 1 - n
            if (s + 1, d, h) in Z:
                go(Z[s + 1, d, h])

    def pass_t(phase, p, s):
        landed(4 * HALF if s == 1 else 4 * QUARTER, tr.at[t_group(phase, p, s)])
        for h, d in HD:
            if s == 1:
                go(T[h, phase, p, 2, d])

    def share(*rs):
        for r in rs:
            go(S[r])

    def split(src, hi, lo, hi8, lo8, first, last):
        def step(i, _):
            rows = pl.ds(pl.multiple_of(first + i * 32, 32), 32)
            v = src[rows, :] * UP
            top = v.astype(BF16)
            rest = v - top.astype(F32)
            hi[rows, :] = top
            lo[rows, :] = rest.astype(BF16)
            hi8[rows, :] = (v * 0.0625).astype(F8)
            lo8[rows, :] = (rest * 16.0).astype(F8)
            return 0

        lax.fori_loop(0, (last - first) // 32, step, 0)

    def split_i(first, last):
        split(img, ih, il, ih8, il8, first, last)

    def split_t(first, last):
        split(txt, th, tl, th8, tl8, first, last)

    def block(i0, i1, t0, t1, first_i=False, first_t=False, across=False, flip=False, hooks=()):
        hooks = dict(enumerate(hooks))
        image = (ih, il, ih8, il8, d_img, rid_i, cid_i, slice(i0, i1), first_i)
        text = (th, tl, th8, tl8, d_txt, rid_t, cid_t, slice(t0, t1), first_t)
        (a_hi, a_lo, a_hi8, a_lo8, d_a, rid, _, ra, first_a) = text if across else image
        (b_hi, b_lo, b_hi8, b_lo8, d_b, _, cid, rb, first_b) = image if across else text
        na, nb = ra.stop - ra.start, rb.stop - rb.start
        s_ref[ra, rb] = dot(jnp.concatenate([a_hi[ra, :], a_lo[ra, :], a_hi[ra, :]], 1),
                            jnp.concatenate([b_hi[rb, :], b_hi[rb, :], b_lo[rb, :]], 1), NT)
        if 0 in hooks:
            hooks[0]()
        n = max(16384 // nb // 32, 1) * 32
        sums = [jnp.zeros((8, nb), F32)] * 3
        for b in range(ra.start, ra.stop, n):
            rows = slice(b, b + n)
            scores = s_ref[rows, rb]
            row = jnp.concatenate([rid[rows, :]] * (nb // 128), 1)
            same = row == jnp.concatenate([cid[:, rb]] * (n // 8), 0)
            losses, slopes = pair_terms(scores, same, warm_down, offset)
            sums = [u + jnp.sum(v.reshape(n // 8, 8, nb), axis=0) for u, v in zip(sums, (losses, slopes * scores, slopes))]
            slopes = slopes * UP
            hi = slopes.astype(BF16)
            sh_ref[rows, rb] = hi
            sh8_ref[rows, rb] = (slopes * 0.0625).astype(F8)
            sl8_ref[rows, rb] = ((slopes - hi.astype(F32)) * 16.0).astype(F8)
        for k, v in enumerate(sums):
            acc[k] += sum(v[:, q:q + 128] for q in range(0, nb, 128))
        if 1 in hooks:
            hooks[1]()
        sh, sh8, sl8 = sh_ref[ra, rb], sh8_ref[ra, rb], sl8_ref[ra, rb]

        def down():
            g = dot(sh, b_hi[rb, :], NN) + dot(jnp.concatenate([sl8, sh8], 1), jnp.concatenate([b_hi8[rb, :], b_lo8[rb, :]], 0), NN)
            d_a[ra, :] = g if first_a else d_a[ra, :] + g

        def over():
            g = dot(sh, a_hi[ra, :], TN) + dot(jnp.concatenate([sl8, sh8], 0), jnp.concatenate([a_hi8[ra, :], a_lo8[ra, :]], 0), TN)
            d_b[rb, :] = g if first_b else d_b[rb, :] + g

        (over if flip else down)()
        if 2 in hooks:
            hooks[2]()
        (down if flip else over)()

    for n in (0, 1):
        for d in (0, 1):
            go(Z[1, d, n if d == 0 else 1 - n])
    for h, d in HD:
        go(T[h, 0, 0, 1, d])
    for h, d in HD:
        go(T[h, 1, 0, 1, d])
    share(0)

    lane = lax.broadcasted_iota(jnp.int32, (8, 128), 1)
    for r in range(NZ):
        number = (((z + NZ - r) % NZ) * NX + x) * (2 * NY) + y * 2
        base = image_row(0, r)
        for k in (0, 1):
            rows = lax.broadcasted_iota(jnp.int32, (SHARD, 128), 0)
            rid_i[base + k * SHARD:base + (k + 1) * SHARD, :] = (number + (c + k) % 2) * SHARD + rows
        own, other = (number + c) * SHARD + lane, (number + (c + 1) % 2) * SHARD + lane - SHARD
        cid_i[:, base:base + 128] = jnp.where(lane < SHARD, own, other)
    for part in range(ROWS // 128):
        ids = jnp.zeros((8, 128), jnp.int32)
        for h in (0, 1):
            for p in range(4):
                for q in range(4):
                    pos = text_row(h, p, q)
                    if pos // 128 == part:
                        a, b = (p, q) if h == 0 else (q, p)
                        number = (((y + NY - b) % NY) * 2 + c) * (NX * NZ) + z * NX + (x + NX - a) % NX
                        off = pos % 128
                        inside = (lane >= off) & (lane < off + HALF)
                        ids = jnp.where(inside, number * SHARD + h * HALF + lane - off, ids)
                        rows = lax.broadcasted_iota(jnp.int32, (HALF, 128), 0)
                        rid_t[pos:pos + HALF, :] = number * SHARD + h * HALF + rows
        cid_t[:, part * 128:(part + 1) * 128] = ids
    acc[...] = jnp.zeros_like(acc)

    pass_t(0, 0, 1)
    for p in (1, 3):
        for h in (0, 1):
            for d in (0, 1):
                go(T[h, 1, p, 1, d])
    pass_z(1, 0)
    landed(SHARD, sr.at[0])
    split_i(0, 128)
    pass_z(1, 1)
    share(1, 7)
    pass_t(0, 0, 2)
    for h in (0, 1):
        for d in (0, 1):
            go(T[h, 1, 2, 1, d])
    split_t(0, 256)
    pass_z(2, 0)
    landed(2 * SHARD, sr.at[1])
    split_i(128, 384)
    pass_t(1, 0, 1)
    pass_t(1, 1, 1)
    split_t(256, 512)

    def nothing():
        pass

    def take(s, n, *rs):
        def hook():
            pass_z(s, n)
            share(*rs)

        return hook

    def take_4():
        landed(2 * HALF, zr.at[6])
        share(4)

    block(0, 256, 0, 512, True, True, hooks=(take(2, 1, 2, 6), nothing, lambda: pass_t(1, 3, 1)))
    landed(2 * SHARD, sr.at[2])
    split_i(384, 640)
    block(256, 512, 0, 512, True, hooks=(take(3, 0), nothing, lambda: pass_t(1, 2, 1)))
    split_t(512, 768)
    block(0, 512, 512, 768, False, True, across=True, hooks=(take(3, 1, 3, 5), nothing, take_4))
    landed(2 * SHARD, sr.at[3])
    split_i(640, 896)
    for p in (0, 1, 3, 2):
        pass_t(1, p, 2)
    split_t(768, 1024)
    landed(SHARD, sr.at[4])
    split_i(896, 1024)
    for k, rows in enumerate((14 * HALF, NZ * SHARD, 15 * SHARD)):
        landed(rows, sent.at[k])

    def rs_copy(r):
        return remote(d_img.at[pl.ds(image_row(1, r), SHARD)], got_s.at[r], sent.at[1], rsr.at[BACK[r]], near["s"])

    def rz_copy(s, d, h):
        r = s if d == 0 else 8 - s
        return remote(d_img.at[pl.ds(image_row(0, r) + h * HALF, HALF)], got_z.at[s - 1, d, pl.ds(h * HALF, HALF)],
                      sent.at[0], rzr.at[z_group(s, 1 - d, h)], near["z-" if d == 0 else "z+"])

    def rt_copy(h, phase, p, s, d):
        q = s if d == 0 else 4 - s
        off, n = (0, HALF) if s < 2 else ((0, QUARTER) if d == 0 else (QUARTER, QUARTER))
        a = text_row(h, q, 0) if phase == 0 else text_row(h, p, q)
        i = t_index(h, phase, p, s, d)
        axis = ("xy", "yx")[h][phase]
        return remote(d_txt.at[pl.ds(a + off, n)], got_t.at[i, pl.ds(0, n)], sent.at[2], rtr.at[t_group(phase, p, s)], near[axis + ("-" if d == 0 else "+")])

    RT = {k: rt_copy(*k) for k in keys}
    RZ = {k: rz_copy(*k) for k in z_keys}
    RS = {r: rs_copy(r) for r in range(NZ)}

    def add_t(h, phase, p, s, d):
        q = s - 1 if d == 0 else (5 - s) % 4
        off, n = (0, HALF) if s < 2 else ((0, QUARTER) if d == 0 else (QUARTER, QUARTER))
        a = (text_row(h, q, 0) if phase == 0 else text_row(h, p, q)) + off
        d_txt[a:a + n, :] += got_t[t_index(h, phase, p, s, d), 0:n, :]

    def add_z(s, d, h):
        r = s - 1 if d == 0 else (9 - s) % 8
        a = image_row(0, r) + h * HALF
        d_img[a:a + HALF, :] += got_z[s - 1, d, h * HALF:(h + 1) * HALF, :]

    def add_s(r):
        a = image_row(0, r)
        d_img[a:a + SHARD, :] += got_s[r]

    def back_t(phase, p, s, then=None):
        landed(4 * HALF if s == 1 else 4 * QUARTER, rtr.at[t_group(phase, p, s)])
        for h, d in HD:
            add_t(h, phase, p, s, d)
            if then is not None:
                go(RT[(h,) + then + (d,)])

    def back_z(s, n):
        landed(2 * HALF, rzr.at[z_group(s, 0, n)])
        for d in (0, 1):
            h = (1 - n if d == 0 else n) if s < 4 else d
            add_z(s, d, h)
            if s > 1:
                go(RZ[s - 1, d, h])

    STAGES = ((0, NZ, lambda k: at(dz=k)), (7, NX, lambda k: at(dx=k)), (10, NY, lambda k: at(dy=k)), (13, 2, lambda k: at(dc=k)))

    def fan(stage):
        base, size, where = STAGES[stage]
        for k in range(1, size):
            go(remote(sum_own.at[stage], sum_got.at[base + k - 1], sent.at[3], qr.at[stage], where(k)))

    def fold(stage):
        base, size, _ = STAGES[stage]
        got = sum_got.at[pl.ds(base, size - 1)]
        pltpu.make_async_copy(got, got, qr.at[stage]).wait()
        total = sum_own[stage]
        for k in range(base, base + size - 1):
            total = total + sum_got[k]
        sum_own[stage + 1] = total

    d_img[512:1024, :] = jnp.zeros((512, D), F32)

    def send_far():
        for p in (2, 1, 3, 0):
            for h, d in HD:
                go(RT[h, 1, p, 2, d])

    block(0, 1024, 768, 1024, False, True, across=True, hooks=(nothing, nothing, send_far))
    for r in (2, 1, 7, 0):
        go(RS[r])

    def send_back():
        for r in (4, 5):
            go(RS[r])

    block(768, 1024, 0, 768, hooks=(nothing, nothing, send_back))

    def start_z():
        landed(2 * SHARD, rsr.at[0])
        add_s(4)
        add_s(5)
        for k in ((4, 0, 0), (4, 1, 1), (3, 1, 0)):
            go(RZ[k])

    def near_t():
        for p in (2, 1, 3, 0):
            back_t(1, p, 2, (1, p, 1))

    block(512, 768, 0, 768, flip=True, hooks=(start_z, nothing, near_t))
    for r in (3, 6):
        go(RS[r])
    for k in range(3):
        sum_own[0, k:k + 1, :] = jnp.sum(acc[k], axis=0, keepdims=True)
    sum_own[0, 3:8, :] = jnp.zeros((5, 128), F32)
    fan(0)
    landed(4 * SHARD, rsr.at[2])
    for r in (2, 1, 7, 0):
        add_s(r)
    landed(2 * SHARD, rsr.at[1])
    for r in (3, 6):
        add_s(r)
    go(RZ[3, 0, 1])
    back_z(4, 0)
    fold(0)
    fan(1)
    back_z(3, 0)
    back_t(1, 2, 1)
    for h, d in HD:
        go(RT[h, 0, 0, 2, d])
    back_z(3, 1)
    fold(1)
    fan(2)
    back_t(1, 1, 1)
    back_z(2, 0)
    back_t(1, 3, 1)
    back_t(0, 0, 2, (0, 0, 1))
    back_z(2, 1)
    fold(2)
    fan(3)
    back_z(1, 0)
    back_t(1, 0, 1)
    back_z(1, 1)
    o_pic[...] = project_back(pic_unit, pic_norm, warm_down * d_img[own_i:own_i + SHARD, :])
    fold(3)
    totals = jnp.sum(sum_own[4], axis=1, keepdims=True) * (1.0 / 16384.0)
    kind = lax.broadcasted_iota(jnp.int32, (8, 1), 0)
    o_sum[...] = jnp.broadcast_to(jnp.where(kind == 1, warm_down * totals, totals), (8, 128))
    back_t(0, 0, 1)
    grads = jnp.concatenate([d_txt[text_row(h, 0, 0):text_row(h, 0, 0) + HALF, :] for h in (0, 1)], 0)
    o_cap[...] = project_back(cap_unit, cap_norm, warm_down * grads)
    for k, rows in enumerate((14 * HALF, NZ * SHARD, 15 * SHARD)):
        landed(rows, sent.at[k])
    pltpu.make_async_copy(sum_got, sum_got, sent.at[3]).wait()


def finish(sums, pic, cap, o_loss, o_pic, o_cap, o_warmth, o_bias):
    o_loss[...] = sums[0:1, 0:1]
    o_warmth[...] = sums[1:2, 0:1]
    o_bias[...] = sums[2:3, 0:1]
    o_pic[...] = pic[...]
    o_cap[...] = cap[...]


def body(picture_vectors, caption_vectors, warmth_exponent, offset_weight):
    vmem, smem, hbm = (pl.BlockSpec(memory_space=m) for m in (pltpu.VMEM, pltpu.SMEM, pl.ANY))
    dma = pltpu.SemaphoreType.DMA
    big, split, eighth = pltpu.VMEM((ROWS, D), F32), pltpu.VMEM((ROWS, D), BF16), pltpu.VMEM((ROWS, D), F8)
    one, shard = jax.ShapeDtypeStruct((1, 1), F32), jax.ShapeDtypeStruct((SHARD, D), F32)
    results = pl.pallas_call(
        kernel,
        out_shape=[jax.ShapeDtypeStruct((8, 128), F32), shard, shard],
        in_specs=[hbm, hbm, smem, smem],
        out_specs=[vmem] * 3,
        scratch_shapes=[
            big, big, split, split, split, split, eighth, eighth, eighth, eighth, big, big,
            pltpu.VMEM((ROWS, ROWS), F32), pltpu.VMEM((ROWS, ROWS), BF16), pltpu.VMEM((ROWS, ROWS), F8), pltpu.VMEM((ROWS, ROWS), F8),
            pltpu.VMEM((ROWS, 128), jnp.int32), pltpu.VMEM((8, ROWS), jnp.int32), pltpu.VMEM((ROWS, 128), jnp.int32),
            pltpu.VMEM((8, ROWS), jnp.int32), pltpu.VMEM((3, 8, 128), F32),
            pltpu.VMEM((NZ, SHARD, D), F32), pltpu.VMEM((4, 2, SHARD, D), F32), pltpu.VMEM((40, HALF, D), F32),
            pltpu.VMEM((5, 8, 128), F32), pltpu.VMEM((14, 8, 128), F32), pltpu.VMEM((SHARD, D), F32), pltpu.VMEM((SHARD, D), F32), dma((2,)),
            dma((7,)), dma((5,)), dma((10,)), dma((7,)), dma((3,)), dma((10,)), dma((4,)), dma((4,)),
        ],
        compiler_params=pltpu.CompilerParams(collective_id=0, has_side_effects=True, vmem_limit_bytes=62 * 2**20),
    )(picture_vectors, caption_vectors, warmth_exponent, offset_weight)
    loss, picture_derivative, caption_derivative, warmth, bias = pl.pallas_call(
        finish, out_shape=[one, shard, shard, one, one], in_specs=[vmem] * 3, out_specs=[vmem] * 5
    )(*results)
    return loss.reshape(1), picture_derivative, caption_derivative, warmth.reshape(1), bias.reshape(1)


def solution(mesh):
    in_specs = (P(("img", "txt"), None), P(("txt", "img"), None), P(), P())
    out_specs = (P(), P(("img", "txt"), None), P(("txt", "img"), None), P(), P())
    return jax.shard_map(body, mesh=mesh, in_specs=in_specs, out_specs=out_specs, check_vma=False)
```

```python
import functools

import jax
import jax.numpy as jnp
from jax import lax
from jax.experimental import pallas as pl
from jax.experimental.pallas import tpu as pltpu
from jax.sharding import PartitionSpec as P

MESH = pl.DeviceIdType.MESH
F32, BF16, F8 = jnp.float32, jnp.bfloat16, jnp.float8_e4m3fn
UP = 4096.0
NX, NY, NZ = 4, 4, 8
SHARD, HALF, QUARTER, D = 64, 32, 16, 1152
ROWS = 1024
SHARE = {0: 0, 1: 1, 7: 1, 2: 2, 6: 2, 3: 3, 5: 3, 4: 4}
BACK = {4: 0, 5: 0, 3: 1, 6: 1, 2: 2, 1: 2, 7: 2, 0: 2}
NT = (((1,), (1,)), ((), ()))
NN = (((1,), (0,)), ((), ()))
TN = (((0,), (0,)), ((), ()))


def dot(a, b, dims):
    return lax.dot_general(a, b, dims, preferred_element_type=F32)


def image_row(k, r):
    return {0: 0, 1: 128, 7: 256, 2: 384, 6: 512, 3: 640, 5: 768, 4: 896}[r] + k * SHARD


def text_row(h, p, q):
    if q == 0:
        at = h * 4 + p
    elif q == 2:
        at = 24 + h * 4 + p
    else:
        at = 8 + (0, 1, 3, 2)[p] * 4 + h * 2 + (q == 3)
    return at * HALF


def unit_rows(values):
    norm = jnp.sqrt(jnp.sum(values * values, axis=1, keepdims=True) + 1e-06)
    return values / norm, norm


def project_back(unit, norm, grads):
    inner = jnp.sum(unit * grads, axis=1, keepdims=True)
    return (grads - unit * inner) / norm


def pair_terms(scores, same, temperature, offset):
    logits = temperature * scores + offset
    g = jnp.exp(jnp.where(same, -logits, logits))
    u = 1.0 + g
    r = pl.reciprocal(u, approx=True)
    part = g * (r * (2.0 - u * r))
    small = g * (1.0 - g * (0.5 - g * (1.0 / 3.0)))
    return jnp.where(g < 0.015625, small, jnp.log(u)), jnp.where(same, -part, part)


def kernel(pic, cap, warmth, bias, o_sum, o_pic, o_cap,
           img, txt, ih, il, th, tl, ih8, il8, th8, tl8, d_img, d_txt, s_ref, sh_ref, sh8_ref, sl8_ref, rid_i, cid_i, rid_t, cid_t, acc,
           got_s, got_z, got_t, sum_own, sum_got, pic_own, cap_own, load, zr, sr, tr, rzr, rsr, rtr, qr, sent):
    loads = [pltpu.make_async_copy(src, dst, load.at[k]) for k, (src, dst) in enumerate(((pic, pic_own), (cap, cap_own)))]
    for copy in loads:
        copy.start()
    im = lax.axis_index("img")
    tx = lax.axis_index("txt")
    z, x = im // NX, im % NX
    y, c = tx // 2, tx % 2

    def at(dx=0, dy=0, dz=0, dc=0):
        return (((z + dz) % NZ) * NX + (x + dx) % NX, ((y + dy) % NY) * 2 + (c + dc) % 2)

    near = {"x+": at(dx=1), "x-": at(dx=3), "y+": at(dy=1), "y-": at(dy=3), "z+": at(dz=1), "z-": at(dz=7), "s": at(dc=1)}
    others = list(near.values()) + [at(dz=k) for k in (2, 3, 4, 5, 6)] + [at(dx=2), at(dy=2)]
    barrier = pltpu.get_barrier_semaphore()
    for other in others:
        pl.semaphore_signal(barrier, inc=1, device_id=other, device_id_type=MESH)

    for copy in loads:
        copy.wait()
    pic_unit, pic_norm = unit_rows(pic_own[...])
    cap_unit, cap_norm = unit_rows(cap_own[...])
    own_i = image_row(0, 0)
    img[own_i:own_i + SHARD, :] = pic_unit
    for h in (0, 1):
        t0 = text_row(h, 0, 0)
        txt[t0:t0 + HALF, :] = cap_unit[h * HALF:(h + 1) * HALF, :]
    temperature = jnp.exp(jnp.full((1, 1), warmth[0], F32))
    offset = jnp.full((1, 1), bias[0], F32)
    warm_down = temperature * (1.0 / (UP * UP))

    pl.semaphore_wait(barrier, len(others))

    def remote(src, dst, s, r, dev):
        return pltpu.make_async_remote_copy(src_ref=src, dst_ref=dst, send_sem=s, recv_sem=r, device_id=dev, device_id_type=MESH)

    def landed(rows, sem):
        pltpu.make_async_copy(d_img.at[pl.ds(0, rows)], d_img.at[pl.ds(0, rows)], sem).wait()

    def go(copy):
        copy.start()

    def z_group(s, d, h):
        return (s - 1) * 2 + ((h if d == 0 else 1 - h) if s < 4 else 0)

    def t_group(phase, p, s):
        return (0 if phase == 0 else 2 + 2 * p) + s - 1

    def z_copy(s, d, h):
        src, dst = ((s - 1), s) if d == 0 else ((9 - s) % 8, 8 - s)
        return remote(img.at[pl.ds(image_row(0, src) + h * HALF, HALF)], img.at[pl.ds(image_row(0, dst) + h * HALF, HALF)],
                      sent.at[0], zr.at[z_group(s, d, h)], near["z+" if d == 0 else "z-"])

    def s_copy(r):
        return remote(img.at[pl.ds(image_row(0, r), SHARD)], img.at[pl.ds(image_row(1, r), SHARD)], sent.at[1], sr.at[SHARE[r]], near["s"])

    def t_index(h, phase, p, s, d):
        return h * 20 + (0 if phase == 0 else 4 + p * 4) + (s - 1) * 2 + d

    def t_copy(h, phase, p, s, d):
        src, dst = (s - 1, s) if d == 0 else ((5 - s) % 4, 4 - s)
        off, n = (0, HALF) if s < 2 else ((0, QUARTER) if d == 0 else (QUARTER, QUARTER))
        a, b = (text_row(h, src, 0), text_row(h, dst, 0)) if phase == 0 else (text_row(h, p, src), text_row(h, p, dst))
        axis = ("xy", "yx")[h][phase]
        return remote(txt.at[pl.ds(a + off, n)], txt.at[pl.ds(b + off, n)], sent.at[2], tr.at[t_group(phase, p, s)], near[axis + ("+" if d == 0 else "-")])

    keys = [(h, 0, 0, s, d) for h in (0, 1) for s in (1, 2) for d in (0, 1)]
    keys += [(h, 1, p, s, d) for h in (0, 1) for p in range(4) for s in (1, 2) for d in (0, 1)]
    z_keys = [(s, d, h) for s in (1, 2, 3) for d in (0, 1) for h in (0, 1)] + [(4, 0, 0), (4, 1, 1)]
    T = {k: t_copy(*k) for k in keys}
    Z = {k: z_copy(*k) for k in z_keys}
    S = {r: s_copy(r) for r in range(NZ)}
    HD = [(h, d) for d in (0, 1) for h in (0, 1)]

    def pass_z(s, n):
        landed(2 * HALF, zr.at[z_group(s, 0, n)])
        for d in (0, 1):
            h = n if d == 0 else 1 - n
            if (s + 1, d, h) in Z:
                go(Z[s + 1, d, h])

    def pass_t(phase, p, s):
        landed(4 * HALF if s == 1 else 4 * QUARTER, tr.at[t_group(phase, p, s)])
        for h, d in HD:
            if s == 1:
                go(T[h, phase, p, 2, d])

    def share(*rs):
        for r in rs:
            go(S[r])

    def split(src, hi, lo, hi8, lo8, first, last):
        def step(i, _):
            rows = pl.ds(pl.multiple_of(first + i * 32, 32), 32)
            v = src[rows, :] * UP
            top = v.astype(BF16)
            rest = v - top.astype(F32)
            hi[rows, :] = top
            lo[rows, :] = rest.astype(BF16)
            hi8[rows, :] = (v * 0.0625).astype(F8)
            lo8[rows, :] = (rest * 16.0).astype(F8)
            return 0

        lax.fori_loop(0, (last - first) // 32, step, 0)

    def split_i(first, last):
        split(img, ih, il, ih8, il8, first, last)

    def split_t(first, last):
        split(txt, th, tl, th8, tl8, first, last)

    def block(i0, i1, t0, t1, first_i=False, first_t=False, across=False, flip=False, hooks=()):
        hooks = dict(enumerate(hooks))
        image = (ih, il, ih8, il8, d_img, rid_i, cid_i, slice(i0, i1), first_i)
        text = (th, tl, th8, tl8, d_txt, rid_t, cid_t, slice(t0, t1), first_t)
        (a_hi, a_lo, a_hi8, a_lo8, d_a, rid, _, ra, first_a) = text if across else image
        (b_hi, b_lo, b_hi8, b_lo8, d_b, _, cid, rb, first_b) = image if across else text
        na, nb = ra.stop - ra.start, rb.stop - rb.start
        s_ref[ra, rb] = dot(jnp.concatenate([a_hi[ra, :], a_lo[ra, :], a_hi[ra, :]], 1),
                            jnp.concatenate([b_hi[rb, :], b_hi[rb, :], b_lo[rb, :]], 1), NT)
        if 0 in hooks:
            hooks[0]()
        n = max(16384 // nb // 32, 1) * 32
        sums = [jnp.zeros((8, nb), F32)] * 3
        for b in range(ra.start, ra.stop, n):
            rows = slice(b, b + n)
            scores = s_ref[rows, rb]
            row = jnp.concatenate([rid[rows, :]] * (nb // 128), 1)
            same = row == jnp.concatenate([cid[:, rb]] * (n // 8), 0)
            losses, slopes = pair_terms(scores, same, warm_down, offset)
            sums = [u + jnp.sum(v.reshape(n // 8, 8, nb), axis=0) for u, v in zip(sums, (losses, slopes * scores, slopes))]
            slopes = slopes * UP
            hi = slopes.astype(BF16)
            sh_ref[rows, rb] = hi
            sh8_ref[rows, rb] = (slopes * 0.0625).astype(F8)
            sl8_ref[rows, rb] = ((slopes - hi.astype(F32)) * 16.0).astype(F8)
        for k, v in enumerate(sums):
            acc[k] += sum(v[:, q:q + 128] for q in range(0, nb, 128))
        if 1 in hooks:
            hooks[1]()
        sh, sh8, sl8 = sh_ref[ra, rb], sh8_ref[ra, rb], sl8_ref[ra, rb]

        def down():
            g = dot(sh, b_hi[rb, :], NN) + dot(jnp.concatenate([sl8, sh8], 1), jnp.concatenate([b_hi8[rb, :], b_lo8[rb, :]], 0), NN)
            d_a[ra, :] = g if first_a else d_a[ra, :] + g

        def over():
            g = dot(sh, a_hi[ra, :], TN) + dot(jnp.concatenate([sl8, sh8], 0), jnp.concatenate([a_hi8[ra, :], a_lo8[ra, :]], 0), TN)
            d_b[rb, :] = g if first_b else d_b[rb, :] + g

        (over if flip else down)()
        if 2 in hooks:
            hooks[2]()
        (down if flip else over)()

    for n in (0, 1):
        for d in (0, 1):
            go(Z[1, d, n if d == 0 else 1 - n])
    for h, d in HD:
        go(T[h, 0, 0, 1, d])
    for h, d in HD:
        go(T[h, 1, 0, 1, d])
    share(0)

    lane = lax.broadcasted_iota(jnp.int32, (8, 128), 1)
    for r in range(NZ):
        number = (((z + NZ - r) % NZ) * NX + x) * (2 * NY) + y * 2
        base = image_row(0, r)
        for k in (0, 1):
            rows = lax.broadcasted_iota(jnp.int32, (SHARD, 128), 0)
            rid_i[base + k * SHARD:base + (k + 1) * SHARD, :] = (number + (c + k) % 2) * SHARD + rows
        own, other = (number + c) * SHARD + lane, (number + (c + 1) % 2) * SHARD + lane - SHARD
        cid_i[:, base:base + 128] = jnp.where(lane < SHARD, own, other)
    for part in range(ROWS // 128):
        ids = jnp.zeros((8, 128), jnp.int32)
        for h in (0, 1):
            for p in range(4):
                for q in range(4):
                    pos = text_row(h, p, q)
                    if pos // 128 == part:
                        a, b = (p, q) if h == 0 else (q, p)
                        number = (((y + NY - b) % NY) * 2 + c) * (NX * NZ) + z * NX + (x + NX - a) % NX
                        off = pos % 128
                        inside = (lane >= off) & (lane < off + HALF)
                        ids = jnp.where(inside, number * SHARD + h * HALF + lane - off, ids)
                        rows = lax.broadcasted_iota(jnp.int32, (HALF, 128), 0)
                        rid_t[pos:pos + HALF, :] = number * SHARD + h * HALF + rows
        cid_t[:, part * 128:(part + 1) * 128] = ids
    acc[...] = jnp.zeros_like(acc)

    pass_t(0, 0, 1)
    for p in (1, 3):
        for h in (0, 1):
            for d in (0, 1):
                go(T[h, 1, p, 1, d])
    pass_z(1, 0)
    landed(SHARD, sr.at[0])
    split_i(0, 128)
    pass_z(1, 1)
    share(1, 7)
    pass_t(0, 0, 2)
    for h in (0, 1):
        for d in (0, 1):
            go(T[h, 1, 2, 1, d])
    split_t(0, 256)
    pass_z(2, 0)
    landed(2 * SHARD, sr.at[1])
    split_i(128, 384)
    pass_t(1, 0, 1)
    pass_t(1, 1, 1)
    split_t(256, 512)

    def nothing():
        pass

    def take(s, n, *rs):
        def hook():
            pass_z(s, n)
            share(*rs)

        return hook

    def take_4():
        landed(2 * HALF, zr.at[6])
        share(4)

    block(0, 256, 0, 512, True, True, hooks=(take(2, 1, 2, 6), nothing, lambda: pass_t(1, 3, 1)))
    landed(2 * SHARD, sr.at[2])
    split_i(384, 640)
    block(256, 512, 0, 512, True, hooks=(take(3, 0), nothing, lambda: pass_t(1, 2, 1)))
    split_t(512, 768)
    block(0, 512, 512, 768, False, True, across=True, hooks=(take(3, 1, 3, 5), nothing, take_4))
    landed(2 * SHARD, sr.at[3])
    split_i(640, 896)
    for p in (0, 1, 3, 2):
        pass_t(1, p, 2)
    split_t(768, 1024)
    landed(SHARD, sr.at[4])
    split_i(896, 1024)
    for k, rows in enumerate((14 * HALF, NZ * SHARD, 15 * SHARD)):
        landed(rows, sent.at[k])

    def rs_copy(r):
        return remote(d_img.at[pl.ds(image_row(1, r), SHARD)], got_s.at[r], sent.at[1], rsr.at[BACK[r]], near["s"])

    def rz_copy(s, d, h):
        r = s if d == 0 else 8 - s
        return remote(d_img.at[pl.ds(image_row(0, r) + h * HALF, HALF)], got_z.at[s - 1, d, pl.ds(h * HALF, HALF)],
                      sent.at[0], rzr.at[z_group(s, 1 - d, h)], near["z-" if d == 0 else "z+"])

    def rt_copy(h, phase, p, s, d):
        q = s if d == 0 else 4 - s
        off, n = (0, HALF) if s < 2 else ((0, QUARTER) if d == 0 else (QUARTER, QUARTER))
        a = text_row(h, q, 0) if phase == 0 else text_row(h, p, q)
        i = t_index(h, phase, p, s, d)
        axis = ("xy", "yx")[h][phase]
        return remote(d_txt.at[pl.ds(a + off, n)], got_t.at[i, pl.ds(0, n)], sent.at[2], rtr.at[t_group(phase, p, s)], near[axis + ("-" if d == 0 else "+")])

    RT = {k: rt_copy(*k) for k in keys}
    RZ = {k: rz_copy(*k) for k in z_keys}
    RS = {r: rs_copy(r) for r in range(NZ)}

    def add_t(h, phase, p, s, d):
        q = s - 1 if d == 0 else (5 - s) % 4
        off, n = (0, HALF) if s < 2 else ((0, QUARTER) if d == 0 else (QUARTER, QUARTER))
        a = (text_row(h, q, 0) if phase == 0 else text_row(h, p, q)) + off
        d_txt[a:a + n, :] += got_t[t_index(h, phase, p, s, d), 0:n, :]

    def add_z(s, d, h):
        r = s - 1 if d == 0 else (9 - s) % 8
        a = image_row(0, r) + h * HALF
        d_img[a:a + HALF, :] += got_z[s - 1, d, h * HALF:(h + 1) * HALF, :]

    def add_s(r):
        a = image_row(0, r)
        d_img[a:a + SHARD, :] += got_s[r]

    def back_t(phase, p, s, then=None):
        landed(4 * HALF if s == 1 else 4 * QUARTER, rtr.at[t_group(phase, p, s)])
        for h, d in HD:
            add_t(h, phase, p, s, d)
            if then is not None:
                go(RT[(h,) + then + (d,)])

    def back_z(s, n):
        landed(2 * HALF, rzr.at[z_group(s, 0, n)])
        for d in (0, 1):
            h = (1 - n if d == 0 else n) if s < 4 else d
            add_z(s, d, h)
            if s > 1:
                go(RZ[s - 1, d, h])

    STAGES = ((0, NZ, lambda k: at(dz=k)), (7, NX, lambda k: at(dx=k)), (10, NY, lambda k: at(dy=k)), (13, 2, lambda k: at(dc=k)))

    def fan(stage):
        base, size, where = STAGES[stage]
        for k in range(1, size):
            go(remote(sum_own.at[stage], sum_got.at[base + k - 1], sent.at[3], qr.at[stage], where(k)))

    def fold(stage):
        base, size, _ = STAGES[stage]
        got = sum_got.at[pl.ds(base, size - 1)]
        pltpu.make_async_copy(got, got, qr.at[stage]).wait()
        total = sum_own[stage]
        for k in range(base, base + size - 1):
            total = total + sum_got[k]
        sum_own[stage + 1] = total

    d_img[512:1024, :] = jnp.zeros((512, D), F32)

    def send_far():
        for p in (2, 1, 3, 0):
            for h, d in HD:
                go(RT[h, 1, p, 2, d])

    block(0, 1024, 768, 1024, False, True, across=True, hooks=(nothing, nothing, send_far))
    for r in (2, 1, 7, 0):
        go(RS[r])

    def send_back():
        for r in (4, 5):
            go(RS[r])

    block(768, 1024, 0, 768, hooks=(nothing, nothing, send_back))

    def start_z():
        landed(2 * SHARD, rsr.at[0])
        add_s(4)
        add_s(5)
        for k in ((4, 0, 0), (4, 1, 1), (3, 1, 0)):
            go(RZ[k])

    def near_t():
        for p in (2, 1, 3):
            back_t(1, p, 2, (1, p, 1))

    def send_next():
        for r in (3, 6):
            go(RS[r])

    block(512, 768, 0, 768, hooks=(start_z, nothing, send_next))
    near_t()
    for k in range(3):
        sum_own[0, k:k + 1, :] = jnp.sum(acc[k], axis=0, keepdims=True)
    sum_own[0, 3:8, :] = jnp.zeros((5, 128), F32)
    fan(0)
    landed(2 * SHARD, rsr.at[1])
    for r in (3, 6):
        add_s(r)
    go(RZ[3, 0, 1])
    back_z(4, 0)
    landed(4 * SHARD, rsr.at[2])
    for r in (2, 1, 7, 0):
        add_s(r)
    fold(0)
    fan(1)
    back_t(1, 2, 1)
    for h, d in HD:
        go(RT[h, 0, 0, 2, d])
    back_t(1, 0, 2, (1, 0, 1))
    back_z(3, 0)
    fold(1)
    fan(2)
    back_t(1, 1, 1)
    back_z(3, 1)
    fold(2)
    fan(3)
    back_t(1, 3, 1)
    back_t(0, 0, 2, (0, 0, 1))
    back_z(2, 0)
    back_z(2, 1)
    back_t(1, 0, 1)
    back_z(1, 0)
    fold(3)
    totals = jnp.sum(sum_own[4], axis=1, keepdims=True) * (1.0 / 16384.0)
    kind = lax.broadcasted_iota(jnp.int32, (8, 1), 0)
    o_sum[...] = jnp.broadcast_to(jnp.where(kind == 1, warm_down * totals, totals), (8, 128))
    back_t(0, 0, 1)
    grads = jnp.concatenate([d_txt[text_row(h, 0, 0):text_row(h, 0, 0) + HALF, :] for h in (0, 1)], 0)
    o_cap[...] = project_back(cap_unit, cap_norm, warm_down * grads)
    back_z(1, 1)
    o_pic[...] = project_back(pic_unit, pic_norm, warm_down * d_img[own_i:own_i + SHARD, :])
    for k, rows in enumerate((14 * HALF, NZ * SHARD, 15 * SHARD)):
        landed(rows, sent.at[k])
    pltpu.make_async_copy(sum_got, sum_got, sent.at[3]).wait()


def finish(sums, pic, cap, o_loss, o_pic, o_cap, o_warmth, o_bias):
    o_loss[...] = sums[0:1, 0:1]
    o_warmth[...] = sums[1:2, 0:1]
    o_bias[...] = sums[2:3, 0:1]
    o_pic[...] = pic[...]
    o_cap[...] = cap[...]


def body(picture_vectors, caption_vectors, warmth_exponent, offset_weight):
    vmem, smem, hbm = (pl.BlockSpec(memory_space=m) for m in (pltpu.VMEM, pltpu.SMEM, pl.ANY))
    dma = pltpu.SemaphoreType.DMA
    big, split, eighth = pltpu.VMEM((ROWS, D), F32), pltpu.VMEM((ROWS, D), BF16), pltpu.VMEM((ROWS, D), F8)
    one, shard = jax.ShapeDtypeStruct((1, 1), F32), jax.ShapeDtypeStruct((SHARD, D), F32)
    results = pl.pallas_call(
        kernel,
        out_shape=[jax.ShapeDtypeStruct((8, 128), F32), shard, shard],
        in_specs=[hbm, hbm, smem, smem],
        out_specs=[vmem] * 3,
        scratch_shapes=[
            big, big, split, split, split, split, eighth, eighth, eighth, eighth, big, big,
            pltpu.VMEM((ROWS, ROWS), F32), pltpu.VMEM((ROWS, ROWS), BF16), pltpu.VMEM((ROWS, ROWS), F8), pltpu.VMEM((ROWS, ROWS), F8),
            pltpu.VMEM((ROWS, 128), jnp.int32), pltpu.VMEM((8, ROWS), jnp.int32), pltpu.VMEM((ROWS, 128), jnp.int32),
            pltpu.VMEM((8, ROWS), jnp.int32), pltpu.VMEM((3, 8, 128), F32),
            pltpu.VMEM((NZ, SHARD, D), F32), pltpu.VMEM((4, 2, SHARD, D), F32), pltpu.VMEM((40, HALF, D), F32),
            pltpu.VMEM((5, 8, 128), F32), pltpu.VMEM((14, 8, 128), F32), pltpu.VMEM((SHARD, D), F32), pltpu.VMEM((SHARD, D), F32), dma((2,)),
            dma((7,)), dma((5,)), dma((10,)), dma((7,)), dma((3,)), dma((10,)), dma((4,)), dma((4,)),
        ],
        compiler_params=pltpu.CompilerParams(collective_id=0, has_side_effects=True, vmem_limit_bytes=62 * 2**20),
    )(picture_vectors, caption_vectors, warmth_exponent, offset_weight)
    loss, picture_derivative, caption_derivative, warmth, bias = pl.pallas_call(
        finish, out_shape=[one, shard, shard, one, one], in_specs=[vmem] * 3, out_specs=[vmem] * 5
    )(*results)
    return loss.reshape(1), picture_derivative, caption_derivative, warmth.reshape(1), bias.reshape(1)


def solution(mesh):
    in_specs = (P(("img", "txt"), None), P(("txt", "img"), None), P(), P())
    out_specs = (P(), P(("img", "txt"), None), P(("txt", "img"), None), P(), P())
    return jax.shard_map(body, mesh=mesh, in_specs=in_specs, out_specs=out_specs, check_vma=False)
```

```python
import functools

import jax
import jax.numpy as jnp
from jax import lax
from jax.experimental import pallas as pl
from jax.experimental.pallas import tpu as pltpu
from jax.sharding import PartitionSpec as P

MESH = pl.DeviceIdType.MESH
F32, BF16, F8 = jnp.float32, jnp.bfloat16, jnp.float8_e4m3fn
UP = 4096.0
NX, NY, NZ = 4, 4, 8
SHARD, HALF, QUARTER, D = 64, 32, 16, 1152
ROWS = 1024
SHARE = {0: 0, 1: 1, 7: 1, 2: 2, 6: 2, 3: 3, 5: 3, 4: 4}
BACK = {4: 0, 5: 0, 3: 1, 6: 1, 2: 2, 1: 2, 7: 2, 0: 2}
NT = (((1,), (1,)), ((), ()))
NN = (((1,), (0,)), ((), ()))
TN = (((0,), (0,)), ((), ()))


def dot(a, b, dims):
    return lax.dot_general(a, b, dims, preferred_element_type=F32)


def image_row(k, r):
    return {0: 0, 1: 128, 7: 256, 2: 384, 6: 512, 3: 640, 5: 768, 4: 896}[r] + k * SHARD


def text_row(h, p, q):
    if q == 0:
        at = h * 4 + p
    elif q == 2:
        at = 24 + h * 4 + p
    else:
        at = 8 + (0, 1, 3, 2)[p] * 4 + h * 2 + (q == 3)
    return at * HALF


def unit_rows(values):
    norm = jnp.sqrt(jnp.sum(values * values, axis=1, keepdims=True) + 1e-06)
    return values / norm, norm


def project_back(unit, norm, grads):
    inner = jnp.sum(unit * grads, axis=1, keepdims=True)
    return (grads - unit * inner) / norm


def pair_terms(scores, same, temperature, offset):
    logits = temperature * scores + offset
    e = jnp.exp(logits)
    u = 1.0 + e
    r = 1.0 / u
    slopes = jnp.where(same, -r, e * r)
    g = jnp.where(same, 1.0 / e, e)
    small = g * (1.0 - g * (0.5 - g * (1.0 / 3.0)))
    losses = jnp.where(g < 0.015625, small, jnp.log(1.0 + g))
    return losses, slopes


def kernel(pic, cap, warmth, bias, o_sum, o_pic, o_cap,
           img, txt, ih, il, th, tl, ih8, il8, th8, tl8, d_img, d_txt, s_ref, sh_ref, sh8_ref, sl8_ref, rid_i, cid_i, rid_t, cid_t, acc,
           got_s, got_z, got_t, sum_own, sum_got, pic_own, cap_own, load, zr, sr, tr, rzr, rsr, rtr, qr, sent):
    loads = [pltpu.make_async_copy(src, dst, load.at[k]) for k, (src, dst) in enumerate(((pic, pic_own), (cap, cap_own)))]
    for copy in loads:
        copy.start()
    im = lax.axis_index("img")
    tx = lax.axis_index("txt")
    z, x = im // NX, im % NX
    y, c = tx // 2, tx % 2

    def at(dx=0, dy=0, dz=0, dc=0):
        return (((z + dz) % NZ) * NX + (x + dx) % NX, ((y + dy) % NY) * 2 + (c + dc) % 2)

    near = {"x+": at(dx=1), "x-": at(dx=3), "y+": at(dy=1), "y-": at(dy=3), "z+": at(dz=1), "z-": at(dz=7), "s": at(dc=1)}
    others = list(near.values()) + [at(dz=k) for k in (2, 3, 4, 5, 6)] + [at(dx=2), at(dy=2)]
    barrier = pltpu.get_barrier_semaphore()
    for other in others:
        pl.semaphore_signal(barrier, inc=1, device_id=other, device_id_type=MESH)

    for copy in loads:
        copy.wait()
    pic_unit, pic_norm = unit_rows(pic_own[...])
    cap_unit, cap_norm = unit_rows(cap_own[...])
    own_i = image_row(0, 0)
    img[own_i:own_i + SHARD, :] = pic_unit
    for h in (0, 1):
        t0 = text_row(h, 0, 0)
        txt[t0:t0 + HALF, :] = cap_unit[h * HALF:(h + 1) * HALF, :]
    temperature = jnp.exp(jnp.full((1, 1), warmth[0], F32))
    offset = jnp.full((1, 1), bias[0], F32)
    warm_down = temperature * (1.0 / (UP * UP))

    pl.semaphore_wait(barrier, len(others))

    def remote(src, dst, s, r, dev):
        return pltpu.make_async_remote_copy(src_ref=src, dst_ref=dst, send_sem=s, recv_sem=r, device_id=dev, device_id_type=MESH)

    def landed(rows, sem):
        pltpu.make_async_copy(d_img.at[pl.ds(0, rows)], d_img.at[pl.ds(0, rows)], sem).wait()

    def go(copy):
        copy.start()

    def z_group(s, d, h):
        return (s - 1) * 2 + ((h if d == 0 else 1 - h) if s < 4 else 0)

    def t_group(phase, p, s):
        return (0 if phase == 0 else 2 + 2 * p) + s - 1

    def z_copy(s, d, h):
        src, dst = ((s - 1), s) if d == 0 else ((9 - s) % 8, 8 - s)
        return remote(img.at[pl.ds(image_row(0, src) + h * HALF, HALF)], img.at[pl.ds(image_row(0, dst) + h * HALF, HALF)],
                      sent.at[0], zr.at[z_group(s, d, h)], near["z+" if d == 0 else "z-"])

    def s_copy(r):
        return remote(img.at[pl.ds(image_row(0, r), SHARD)], img.at[pl.ds(image_row(1, r), SHARD)], sent.at[1], sr.at[SHARE[r]], near["s"])

    def t_index(h, phase, p, s, d):
        return h * 20 + (0 if phase == 0 else 4 + p * 4) + (s - 1) * 2 + d

    def t_copy(h, phase, p, s, d):
        src, dst = (s - 1, s) if d == 0 else ((5 - s) % 4, 4 - s)
        off, n = (0, HALF) if s < 2 else ((0, QUARTER) if d == 0 else (QUARTER, QUARTER))
        a, b = (text_row(h, src, 0), text_row(h, dst, 0)) if phase == 0 else (text_row(h, p, src), text_row(h, p, dst))
        axis = ("xy", "yx")[h][phase]
        return remote(txt.at[pl.ds(a + off, n)], txt.at[pl.ds(b + off, n)], sent.at[2], tr.at[t_group(phase, p, s)], near[axis + ("+" if d == 0 else "-")])

    keys = [(h, 0, 0, s, d) for h in (0, 1) for s in (1, 2) for d in (0, 1)]
    keys += [(h, 1, p, s, d) for h in (0, 1) for p in range(4) for s in (1, 2) for d in (0, 1)]
    z_keys = [(s, d, h) for s in (1, 2, 3) for d in (0, 1) for h in (0, 1)] + [(4, 0, 0), (4, 1, 1)]
    T = {k: t_copy(*k) for k in keys}
    Z = {k: z_copy(*k) for k in z_keys}
    S = {r: s_copy(r) for r in range(NZ)}
    HD = [(h, d) for d in (0, 1) for h in (0, 1)]

    def pass_z(s, n):
        landed(2 * HALF, zr.at[z_group(s, 0, n)])
        for d in (0, 1):
            h = n if d == 0 else 1 - n
            if (s + 1, d, h) in Z:
                go(Z[s + 1, d, h])

    def pass_t(phase, p, s):
        landed(4 * HALF if s == 1 else 4 * QUARTER, tr.at[t_group(phase, p, s)])
        for h, d in HD:
            if s == 1:
                go(T[h, phase, p, 2, d])

    def share(*rs):
        for r in rs:
            go(S[r])

    def split(src, hi, lo, hi8, lo8, first, last):
        def step(i, _):
            rows = pl.ds(pl.multiple_of(first + i * 32, 32), 32)
            v = src[rows, :] * UP
            top = v.astype(BF16)
            rest = v - top.astype(F32)
            hi[rows, :] = top
            lo[rows, :] = rest.astype(BF16)
            hi8[rows, :] = (v * 0.0625).astype(F8)
            lo8[rows, :] = (rest * 16.0).astype(F8)
            return 0

        lax.fori_loop(0, (last - first) // 32, step, 0)

    def split_i(first, last):
        split(img, ih, il, ih8, il8, first, last)

    def split_t(first, last):
        split(txt, th, tl, th8, tl8, first, last)

    def block(i0, i1, t0, t1, first_i=False, first_t=False, across=False, flip=False, hooks=()):
        hooks = dict(enumerate(hooks))
        image = (ih, il, ih8, il8, d_img, rid_i, cid_i, slice(i0, i1), first_i)
        text = (th, tl, th8, tl8, d_txt, rid_t, cid_t, slice(t0, t1), first_t)
        (a_hi, a_lo, a_hi8, a_lo8, d_a, rid, _, ra, first_a) = text if across else image
        (b_hi, b_lo, b_hi8, b_lo8, d_b, _, cid, rb, first_b) = image if across else text
        na, nb = ra.stop - ra.start, rb.stop - rb.start
        s_ref[ra, rb] = dot(jnp.concatenate([a_hi[ra, :], a_lo[ra, :], a_hi[ra, :]], 1),
                            jnp.concatenate([b_hi[rb, :], b_hi[rb, :], b_lo[rb, :]], 1), NT)
        if 0 in hooks:
            hooks[0]()
        n = max(16384 // nb // 32, 1) * 32
        sums = [jnp.zeros((8, nb), F32)] * 3
        for b in range(ra.start, ra.stop, n):
            rows = slice(b, b + n)
            scores = s_ref[rows, rb]
            row = jnp.concatenate([rid[rows, :]] * (nb // 128), 1)
            same = row == jnp.concatenate([cid[:, rb]] * (n // 8), 0)
            losses, slopes = pair_terms(scores, same, warm_down, offset)
            sums = [u + jnp.sum(v.reshape(n // 8, 8, nb), axis=0) for u, v in zip(sums, (losses, slopes * scores, slopes))]
            slopes = slopes * UP
            hi = slopes.astype(BF16)
            sh_ref[rows, rb] = hi
            sh8_ref[rows, rb] = (slopes * 0.0625).astype(F8)
            sl8_ref[rows, rb] = ((slopes - hi.astype(F32)) * 16.0).astype(F8)
        for k, v in enumerate(sums):
            acc[k] += sum(v[:, q:q + 128] for q in range(0, nb, 128))
        if 1 in hooks:
            hooks[1]()
        sh, sh8, sl8 = sh_ref[ra, rb], sh8_ref[ra, rb], sl8_ref[ra, rb]

        def down():
            g = dot(sh, b_hi[rb, :], NN) + dot(jnp.concatenate([sl8, sh8], 1), jnp.concatenate([b_hi8[rb, :], b_lo8[rb, :]], 0), NN)
            d_a[ra, :] = g if first_a else d_a[ra, :] + g

        def over():
            g = dot(sh, a_hi[ra, :], TN) + dot(jnp.concatenate([sl8, sh8], 0), jnp.concatenate([a_hi8[ra, :], a_lo8[ra, :]], 0), TN)
            d_b[rb, :] = g if first_b else d_b[rb, :] + g

        (over if flip else down)()
        if 2 in hooks:
            hooks[2]()
        (down if flip else over)()

    for n in (0, 1):
        for d in (0, 1):
            go(Z[1, d, n if d == 0 else 1 - n])
    for h, d in HD:
        go(T[h, 0, 0, 1, d])
    for h, d in HD:
        go(T[h, 1, 0, 1, d])
    share(0)

    lane = lax.broadcasted_iota(jnp.int32, (8, 128), 1)
    for r in range(NZ):
        number = (((z + NZ - r) % NZ) * NX + x) * (2 * NY) + y * 2
        base = image_row(0, r)
        for k in (0, 1):
            rows = lax.broadcasted_iota(jnp.int32, (SHARD, 128), 0)
            rid_i[base + k * SHARD:base + (k + 1) * SHARD, :] = (number + (c + k) % 2) * SHARD + rows
        own, other = (number + c) * SHARD + lane, (number + (c + 1) % 2) * SHARD + lane - SHARD
        cid_i[:, base:base + 128] = jnp.where(lane < SHARD, own, other)
    for part in range(ROWS // 128):
        ids = jnp.zeros((8, 128), jnp.int32)
        for h in (0, 1):
            for p in range(4):
                for q in range(4):
                    pos = text_row(h, p, q)
                    if pos // 128 == part:
                        a, b = (p, q) if h == 0 else (q, p)
                        number = (((y + NY - b) % NY) * 2 + c) * (NX * NZ) + z * NX + (x + NX - a) % NX
                        off = pos % 128
                        inside = (lane >= off) & (lane < off + HALF)
                        ids = jnp.where(inside, number * SHARD + h * HALF + lane - off, ids)
                        rows = lax.broadcasted_iota(jnp.int32, (HALF, 128), 0)
                        rid_t[pos:pos + HALF, :] = number * SHARD + h * HALF + rows
        cid_t[:, part * 128:(part + 1) * 128] = ids
    acc[...] = jnp.zeros_like(acc)

    pass_t(0, 0, 1)
    for p in (1, 3):
        for h in (0, 1):
            for d in (0, 1):
                go(T[h, 1, p, 1, d])
    pass_z(1, 0)
    landed(SHARD, sr.at[0])
    split_i(0, 128)
    pass_z(1, 1)
    share(1, 7)
    pass_t(0, 0, 2)
    for h in (0, 1):
        for d in (0, 1):
            go(T[h, 1, 2, 1, d])
    split_t(0, 256)
    pass_z(2, 0)
    landed(2 * SHARD, sr.at[1])
    split_i(128, 384)
    pass_t(1, 0, 1)
    pass_t(1, 1, 1)
    split_t(256, 512)

    def nothing():
        pass

    def take(s, n, *rs):
        def hook():
            pass_z(s, n)
            share(*rs)

        return hook

    def take_4():
        landed(2 * HALF, zr.at[6])
        share(4)

    block(0, 256, 0, 512, True, True, hooks=(take(2, 1, 2, 6), nothing, lambda: pass_t(1, 3, 1)))
    landed(2 * SHARD, sr.at[2])
    split_i(384, 640)
    block(256, 512, 0, 512, True, hooks=(take(3, 0), nothing, lambda: pass_t(1, 2, 1)))
    split_t(512, 768)
    block(0, 512, 512, 768, False, True, across=True, hooks=(take(3, 1, 3, 5),))
    landed(2 * SHARD, sr.at[3])
    split_i(640, 896)
    block(512, 768, 0, 512, True, hooks=(nothing, take_4))
    for p in (0, 1, 3, 2):
        pass_t(1, p, 2)
    split_t(768, 1024)
    landed(SHARD, sr.at[4])
    split_i(896, 1024)
    for k, rows in enumerate((14 * HALF, NZ * SHARD, 15 * SHARD)):
        landed(rows, sent.at[k])

    def rs_copy(r):
        return remote(d_img.at[pl.ds(image_row(1, r), SHARD)], got_s.at[r], sent.at[1], rsr.at[BACK[r]], near["s"])

    def rz_copy(s, d, h):
        r = s if d == 0 else 8 - s
        return remote(d_img.at[pl.ds(image_row(0, r) + h * HALF, HALF)], got_z.at[s - 1, d, pl.ds(h * HALF, HALF)],
                      sent.at[0], rzr.at[z_group(s, 1 - d, h)], near["z-" if d == 0 else "z+"])

    def rt_copy(h, phase, p, s, d):
        q = s if d == 0 else 4 - s
        off, n = (0, HALF) if s < 2 else ((0, QUARTER) if d == 0 else (QUARTER, QUARTER))
        a = text_row(h, q, 0) if phase == 0 else text_row(h, p, q)
        i = t_index(h, phase, p, s, d)
        axis = ("xy", "yx")[h][phase]
        return remote(d_txt.at[pl.ds(a + off, n)], got_t.at[i, pl.ds(0, n)], sent.at[2], rtr.at[t_group(phase, p, s)], near[axis + ("-" if d == 0 else "+")])

    RT = {k: rt_copy(*k) for k in keys}
    RZ = {k: rz_copy(*k) for k in z_keys}
    RS = {r: rs_copy(r) for r in range(NZ)}

    def add_t(h, phase, p, s, d):
        q = s - 1 if d == 0 else (5 - s) % 4
        off, n = (0, HALF) if s < 2 else ((0, QUARTER) if d == 0 else (QUARTER, QUARTER))
        a = (text_row(h, q, 0) if phase == 0 else text_row(h, p, q)) + off
        d_txt[a:a + n, :] += got_t[t_index(h, phase, p, s, d), 0:n, :]

    def add_z(s, d, h):
        r = s - 1 if d == 0 else (9 - s) % 8
        a = image_row(0, r) + h * HALF
        d_img[a:a + HALF, :] += got_z[s - 1, d, h * HALF:(h + 1) * HALF, :]

    def add_s(r):
        a = image_row(0, r)
        d_img[a:a + SHARD, :] += got_s[r]

    def back_t(phase, p, s, then=None):
        landed(4 * HALF if s == 1 else 4 * QUARTER, rtr.at[t_group(phase, p, s)])
        for h, d in HD:
            add_t(h, phase, p, s, d)
            if then is not None:
                go(RT[(h,) + then + (d,)])

    def back_z(s, n):
        landed(2 * HALF, rzr.at[z_group(s, 0, n)])
        for d in (0, 1):
            h = (1 - n if d == 0 else n) if s < 4 else d
            add_z(s, d, h)
            if s > 1:
                go(RZ[s - 1, d, h])

    STAGES = ((0, NZ, lambda k: at(dz=k)), (7, NX, lambda k: at(dx=k)), (10, NY, lambda k: at(dy=k)), (13, 2, lambda k: at(dc=k)))

    def fan(stage):
        base, size, where = STAGES[stage]
        for k in range(1, size):
            go(remote(sum_own.at[stage], sum_got.at[base + k - 1], sent.at[3], qr.at[stage], where(k)))

    def fold(stage):
        base, size, _ = STAGES[stage]
        got = sum_got.at[pl.ds(base, size - 1)]
        pltpu.make_async_copy(got, got, qr.at[stage]).wait()
        total = sum_own[stage]
        for k in range(base, base + size - 1):
            total = total + sum_got[k]
        sum_own[stage + 1] = total

    d_img[768:1024, :] = jnp.zeros((256, D), F32)

    def send_far():
        for p in (2, 1, 3, 0):
            for h, d in HD:
                go(RT[h, 1, p, 2, d])

    block(0, 1024, 768, 1024, False, True, across=True, hooks=(nothing, nothing, send_far))
    for r in (2, 1, 7, 0):
        go(RS[r])

    def send_back():
        for r in (4, 5):
            go(RS[r])

    block(768, 1024, 0, 768, hooks=(nothing, nothing, send_back))

    def start_z():
        landed(2 * SHARD, rsr.at[0])
        add_s(4)
        add_s(5)
        for k in ((4, 0, 0), (4, 1, 1), (3, 1, 0)):
            go(RZ[k])

    def near_t():
        for p in (2, 1, 3):
            back_t(1, p, 2, (1, p, 1))

    block(512, 768, 512, 768, flip=True, hooks=(start_z, nothing, near_t))
    for r in (3, 6):
        go(RS[r])
    for k in range(3):
        sum_own[0, k:k + 1, :] = jnp.sum(acc[k], axis=0, keepdims=True)
    sum_own[0, 3:8, :] = jnp.zeros((5, 128), F32)
    fan(0)
    landed(2 * SHARD, rsr.at[1])
    for r in (3, 6):
        add_s(r)
    go(RZ[3, 0, 1])
    back_z(4, 0)
    landed(4 * SHARD, rsr.at[2])
    for r in (2, 1, 7, 0):
        add_s(r)
    fold(0)
    fan(1)
    back_t(1, 2, 1)
    for h, d in HD:
        go(RT[h, 0, 0, 2, d])
    back_t(1, 0, 2, (1, 0, 1))
    back_z(3, 0)
    fold(1)
    fan(2)
    back_t(1, 1, 1)
    back_z(3, 1)
    fold(2)
    fan(3)
    back_t(1, 3, 1)
    back_t(0, 0, 2, (0, 0, 1))
    back_z(2, 0)
    back_z(2, 1)
    back_t(1, 0, 1)
    back_z(1, 0)
    fold(3)
    totals = jnp.sum(sum_own[4], axis=1, keepdims=True) * (1.0 / 16384.0)
    kind = lax.broadcasted_iota(jnp.int32, (8, 1), 0)
    o_sum[...] = jnp.broadcast_to(jnp.where(kind == 1, warm_down * totals, totals), (8, 128))
    back_t(0, 0, 1)
    grads = jnp.concatenate([d_txt[text_row(h, 0, 0):text_row(h, 0, 0) + HALF, :] for h in (0, 1)], 0)
    o_cap[...] = project_back(cap_unit, cap_norm, warm_down * grads)
    back_z(1, 1)
    o_pic[...] = project_back(pic_unit, pic_norm, warm_down * d_img[own_i:own_i + SHARD, :])
    for k, rows in enumerate((14 * HALF, NZ * SHARD, 15 * SHARD)):
        landed(rows, sent.at[k])
    pltpu.make_async_copy(sum_got, sum_got, sent.at[3]).wait()


def finish(sums, pic, cap, o_loss, o_pic, o_cap, o_warmth, o_bias):
    o_loss[...] = sums[0:1, 0:1]
    o_warmth[...] = sums[1:2, 0:1]
    o_bias[...] = sums[2:3, 0:1]
    o_pic[...] = pic[...]
    o_cap[...] = cap[...]


def body(picture_vectors, caption_vectors, warmth_exponent, offset_weight):
    vmem, smem, hbm = (pl.BlockSpec(memory_space=m) for m in (pltpu.VMEM, pltpu.SMEM, pl.ANY))
    dma = pltpu.SemaphoreType.DMA
    big, split, eighth = pltpu.VMEM((ROWS, D), F32), pltpu.VMEM((ROWS, D), BF16), pltpu.VMEM((ROWS, D), F8)
    one, shard = jax.ShapeDtypeStruct((1, 1), F32), jax.ShapeDtypeStruct((SHARD, D), F32)
    results = pl.pallas_call(
        kernel,
        out_shape=[jax.ShapeDtypeStruct((8, 128), F32), shard, shard],
        in_specs=[hbm, hbm, smem, smem],
        out_specs=[vmem] * 3,
        scratch_shapes=[
            big, big, split, split, split, split, eighth, eighth, eighth, eighth, big, big,
            pltpu.VMEM((ROWS, ROWS), F32), pltpu.VMEM((ROWS, ROWS), BF16), pltpu.VMEM((ROWS, ROWS), F8), pltpu.VMEM((ROWS, ROWS), F8),
            pltpu.VMEM((ROWS, 128), jnp.int32), pltpu.VMEM((8, ROWS), jnp.int32), pltpu.VMEM((ROWS, 128), jnp.int32),
            pltpu.VMEM((8, ROWS), jnp.int32), pltpu.VMEM((3, 8, 128), F32),
            pltpu.VMEM((NZ, SHARD, D), F32), pltpu.VMEM((4, 2, SHARD, D), F32), pltpu.VMEM((40, HALF, D), F32),
            pltpu.VMEM((5, 8, 128), F32), pltpu.VMEM((14, 8, 128), F32), pltpu.VMEM((SHARD, D), F32), pltpu.VMEM((SHARD, D), F32), dma((2,)),
            dma((7,)), dma((5,)), dma((10,)), dma((7,)), dma((3,)), dma((10,)), dma((4,)), dma((4,)),
        ],
        compiler_params=pltpu.CompilerParams(collective_id=0, has_side_effects=True, vmem_limit_bytes=62 * 2**20),
    )(picture_vectors, caption_vectors, warmth_exponent, offset_weight)
    loss, picture_derivative, caption_derivative, warmth, bias = pl.pallas_call(
        finish, out_shape=[one, shard, shard, one, one], in_specs=[vmem] * 3, out_specs=[vmem] * 5
    )(*results)
    return loss.reshape(1), picture_derivative, caption_derivative, warmth.reshape(1), bias.reshape(1)


def solution(mesh):
    in_specs = (P(("img", "txt"), None), P(("txt", "img"), None), P(), P())
    out_specs = (P(), P(("img", "txt"), None), P(("txt", "img"), None), P(), P())
    return jax.shard_map(body, mesh=mesh, in_specs=in_specs, out_specs=out_specs, check_vma=False)
```
